512 devices in a mesh: grp: 4 (over z_lo), blk: 32 (over x, y, core), head: 4 (over z_hi).
Axes of the slice: x: 4, y: 4, z: 16 (z_hi: 4, z_lo: 4; z = z_hi * 4 + z_lo), core: 2. Of those that a mesh axis runs over, the one named last changes fastest.
Arguments:
- queries: bfloat16 [65536, 1024], P(('grp', 'blk', 'head')), may hold values from -6 to 6
- keys: bfloat16 [65536, 1024], P(('grp', 'blk', 'head')), may hold values from -6 to 6
- values: bfloat16 [65536, 1024], P(('grp', 'blk', 'head')), may hold values from -6 to 6
- out_grad: bfloat16 [65536, 1024], P(('grp', 'blk', 'head')), may hold values from -6 to 6
- segment: int32 [65536], P(('grp', 'blk', 'head')), may hold values from 0 to 63, never falling along the last dimension, each value on 1 to 2048 neighbouring positions
Outputs:
- attention_out: bfloat16 [65536, 1024], P(('grp', 'blk', 'head'))
- query_grad: bfloat16 [65536, 1024], P(('grp', 'blk', 'head'))
- key_grad: bfloat16 [65536, 1024], P(('grp', 'blk', 'head'))
- value_grad: bfloat16 [65536, 1024], P(('grp', 'blk', 'head'))
The draws below stay inside these ranges and needn't reach their ends.
Inputs may be any that keep to these rules, and one draw needn't show every extreme that they name: `segment`: never falls along the pack; every stream covers 1 to 2048 consecutive positions and one covers exactly 2048.
All inputs are finite; a program needn't handle non-finite values.
Results may differ from the reference program's by a relative error of at most 0.0049.
Values may be sent and summed in bfloat16 or wider, within the bound.
A program may use at most 64 MiB of HBM per device.

```python
import math
import jax
import jax.numpy as jnp
import numpy as np
from jax import lax

TOK_DEV = 128
HEADS = 8
DH = 128
REACH = 4
MAXLEN = 2048
SEQ = 65536
STREAMS = 64
FEAT = 1024
N_HEAD = 4


def levels(key, shape, split, low, largest):
    def one(dim, shards_of):
        steps = jax.random.uniform(jax.random.fold_in(jax.random.fold_in(key, 6), dim), (shards_of,), jnp.float32, low / len(split), largest / len(split))
        return jnp.repeat(jnp.exp(steps), shape[dim] // shards_of).reshape((-1,) + (1,) * (len(shape) - dim - 1))

    gain = one(*split[0])
    for cut in split[1:]:
        gain = gain * one(*cut)
    return gain


def length_profile(number_of, total, bound, lean):
    weights = [(1 << 20) // math.isqrt(rank ** lean) + 1 for rank in range(2, number_of + 1)]
    surplus, given = total - bound - (number_of - 1), [1] * (number_of - 1)
    while surplus > 0:
        free = [i for i in range(number_of - 1) if given[i] < bound]
        whole, budget = sum([weights[i] for i in free]), surplus
        for i in free:
            addition = min(bound - given[i], max(1, budget * weights[i] // whole), surplus)
            given[i] = given[i] + addition
            surplus = surplus - addition
    return np.array([bound] + given)


def ragged(stream_key, count, total, most, skew):
    if count == 2:
        one = jax.random.randint(stream_key, (), max(1, total - most), min(most, total - 1) + 1)
        return jnp.stack([one, total - one])
    tallies = jnp.asarray(length_profile(count, total, most, skew), jnp.int32)
    couples = (count - 1) // 2
    giver, sink = tallies[1:1 + 2 * couples:2], tallies[2:2 + 2 * couples:2]
    room = jnp.minimum(giver - 1, most - sink)
    passed = jax.random.randint(jax.random.fold_in(stream_key, 1), (couples,), 0, 1 << 20) % (room + 1)
    tallies = tallies.at[1:1 + 2 * couples:2].set(giver - passed).at[2:2 + 2 * couples:2].set(sink + passed)
    return tallies[jax.random.permutation(jax.random.fold_in(stream_key, 2), count)]


def scatter_about(stream_key, extent, scale, most, split=(), kind=jnp.bfloat16):
    values = jax.random.normal(stream_key, extent, jnp.float32) * scale
    if len(split) > 0:
        values = levels(stream_key, extent, split, -0.22, 0.18) * values
    return jnp.clip(values, min=-most, max=most).astype(kind)


def setup_inputs(seed: int = 0) -> dict:
    seeds = jax.random.split(jax.random.key(seed), 6)
    queries = scatter_about(seeds[0], (SEQ, FEAT), 1.0, 6.0, ((0, 512),))
    keys = scatter_about(seeds[1], (SEQ, FEAT), 1.0, 6.0, ((0, 512),))
    values = scatter_about(seeds[2], (SEQ, FEAT), 1.0, 6.0, ((0, 512),))
    out_grad = scatter_about(seeds[3], (SEQ, FEAT), 1.0, 6.0, ((0, 512),))
    segment = jnp.searchsorted(jnp.cumsum(ragged(seeds[4], STREAMS, SEQ, MAXLEN, 2)), jnp.arange(SEQ), side="right").astype(jnp.int32)
    return dict(queries=queries, keys=keys, values=values, out_grad=out_grad, segment=segment)


def silu_parts(scores):
    logistic = jax.nn.sigmoid(scores)
    return (scores * logistic, logistic * (1.0 + scores * (1.0 - logistic)))

def reference(queries, keys, values, out_grad, segment):
    block_rows = N_HEAD * TOK_DEV
    block_count = SEQ // block_rows
    margin = REACH * block_rows
    window = margin + block_rows
    width = HEADS * DH
    score_scale = 1.0 / math.sqrt(DH)
    norm_factor = 1.0 / math.sqrt(MAXLEN)
    keys_padded = jnp.concatenate([jnp.zeros((margin, width), keys.dtype), keys], axis=0)
    values_padded = jnp.concatenate([jnp.zeros((margin, width), values.dtype), values], axis=0)
    seg_padded = jnp.concatenate([jnp.full((margin,), -1, jnp.int32), segment.astype(jnp.int32)], axis=0)
    causal = jnp.arange(window, dtype=jnp.int32)[None, :] <= jnp.arange(block_rows, dtype=jnp.int32)[:, None] + margin

    def split_heads(matrix):
        return matrix.reshape(matrix.shape[0], HEADS, DH).astype(jnp.float32)

    def one_block(carry, index):
        key_acc, value_acc = carry
        start = (index * block_rows).astype(jnp.int32)
        query = split_heads(lax.dynamic_slice_in_dim(queries, start, block_rows, 0))
        cotangent = split_heads(lax.dynamic_slice_in_dim(out_grad, start, block_rows, 0))
        seg_query = lax.dynamic_slice_in_dim(segment.astype(jnp.int32), start, block_rows, 0)
        key_block = split_heads(lax.dynamic_slice_in_dim(keys_padded, start, window, 0))
        value_block = split_heads(lax.dynamic_slice_in_dim(values_padded, start, window, 0))
        seg_key = lax.dynamic_slice_in_dim(seg_padded, start, window, 0)
        allowed = (seg_query[:, None] == seg_key[None, :]) & causal
        scores = jnp.einsum('qhd,khd->hqk', query, key_block) * score_scale
        active, slope = silu_parts(scores)
        weight = jnp.where(allowed[None], active * norm_factor, 0.0).astype(jnp.bfloat16)
        weight = lax.optimization_barrier(weight).astype(jnp.float32)
        dprob = jnp.einsum('qhd,khd->hqk', cotangent, value_block)
        dscore = jnp.where(allowed[None], dprob * slope * (norm_factor * score_scale), 0.0).astype(jnp.bfloat16)
        dscore = lax.optimization_barrier(dscore).astype(jnp.float32)
        output = jnp.einsum('hqk,khd->qhd', weight, value_block).reshape(block_rows, width)
        query_term = jnp.einsum('hqk,khd->qhd', dscore, key_block).reshape(block_rows, width)
        key_term = jnp.einsum('hqk,qhd->khd', dscore, query).reshape(window, width)
        value_term = jnp.einsum('hqk,qhd->khd', weight, cotangent).reshape(window, width)
        key_acc = lax.dynamic_update_slice_in_dim(key_acc, lax.dynamic_slice_in_dim(key_acc, start, window, 0) + key_term, start, 0)
        value_acc = lax.dynamic_update_slice_in_dim(value_acc, lax.dynamic_slice_in_dim(value_acc, start, window, 0) + value_term, start, 0)
        return ((key_acc, value_acc), (output.astype(jnp.bfloat16), query_term.astype(jnp.bfloat16)))
    start_acc = jnp.zeros((margin + SEQ, width), jnp.float32)
    (key_acc, value_acc), (outputs, query_terms) = lax.scan(one_block, (start_acc, start_acc), jnp.arange(block_count, dtype=jnp.int32))
    attention_out = outputs.reshape(SEQ, width)
    query_grad = query_terms.reshape(SEQ, width)
    key_grad = key_acc[margin:].astype(jnp.bfloat16)
    value_grad = value_acc[margin:].astype(jnp.bfloat16)
    return (attention_out, query_grad, key_grad, value_grad)
```

```python
import functools
import math

import jax
import jax.numpy as jnp
from jax import lax
from jax.experimental import pallas as pl
from jax.experimental.pallas import tpu as pltpu
from jax.sharding import PartitionSpec as P

MESH = pl.DeviceIdType.MESH
DH = 128
REACH = 4
TOK = 128
PLANES = 4
BLOCK = TOK * PLANES
CHUNK = 2 * TOK + 16
ROWS = 256
NT = (((1,), (1,)), ((), ()))
NN = (((1,), (0,)), ((), ()))


def chip_at(grp, blk, by, blks, grps):
    chips = blks // 2
    chip = lax.rem(grp * chips + blk // 2 + by + chips * grps, chips * grps)
    return chip // chips, lax.rem(chip, chips) * 2 + lax.rem(blk, 2)


def kernel(
    sizes,
    queries, keys, values, out_grad, segment,
    out, query_grad, key_grad, value_grad,
    held, stage, result, acc, seg_rows,
    load_sem, in_send, in_recv, halo_send, halo_recv, sib_send, sib_recv, out_send, out_recv, own_sem,
):
    grps, blks = sizes
    grp, blk, me = lax.axis_index("grp"), lax.axis_index("blk"), lax.axis_index("head")
    core = lax.rem(blk, 2)
    sibling = (grp, blk + 1 - 2 * core, me)
    planes = [lax.rem(me + by, PLANES) for by in range(PLANES)]

    def along(by):
        g, b = chip_at(grp, blk, by, blks, grps)
        return (g, b, me)

    sources = ((keys, values), (queries, out_grad))
    groups = ((0, 0), (0, 1), (1, 0), (1, 1))

    def load(phase, group):
        copies = []
        for by in range(PLANES):
            plane = planes[by]
            column = pl.ds(pl.multiple_of((2 * plane + phase) * DH, DH), DH)
            for a in range(2):
                if by == 0:
                    to = held.at[phase, group, 0, me, pl.ds(a * TOK, TOK)]
                else:
                    to = stage.at[phase, group, by - 1, pl.ds(a * TOK, TOK)]
                copies.append(
                    pltpu.make_async_copy(
                        sources[group][a].at[:, column], to, load_sem.at[phase, group, by, a]
                    )
                )
        return copies

    loads = {pg: load(*pg) for pg in groups}
    for pg in groups:
        for copy in loads[pg]:
            copy.start()

    barrier = pltpu.get_barrier_semaphore()
    partners = [(grp, blk, planes[by]) for by in (1, 2, 3)]
    partners += [sibling] + [along(by) for by in (1, -1, 2, -2)]
    for partner in partners:
        pl.semaphore_signal(barrier, inc=1, device_id=partner, device_id_type=MESH)

    seg = jnp.broadcast_to(segment[...].astype(jnp.float32), (16, TOK)).astype(jnp.bfloat16)
    for by in range(3):
        stage[0, 0, by, 2 * TOK :, :] = seg
    held[0, 0, 0, me, 2 * TOK :, :] = seg

    pl.semaphore_wait(barrier, len(partners))

    def rows_sent(phase, group):
        return CHUNK if (phase, group) == (0, 0) else 2 * TOK

    def exchange(phase, group):
        rows = pl.ds(0, rows_sent(phase, group))
        return [
            pltpu.make_async_remote_copy(
                src_ref=stage.at[phase, group, by - 1, rows],
                dst_ref=held.at[phase, group, 0, me, rows],
                send_sem=in_send.at[phase, group, by - 1],
                recv_sem=in_recv.at[phase, group, by - 1],
                device_id=(grp, blk, planes[by]),
                device_id_type=MESH,
            )
            for by in (2, 1, 3)
        ]

    def halo(phase, group):
        rows = pl.ds(0, CHUNK if phase == 0 else 2 * TOK)
        way = 1 - 2 * group
        return [
            pltpu.make_async_remote_copy(
                src_ref=held.at[phase, group, 0, :, rows],
                dst_ref=held.at[phase, group, 2 * by, :, rows],
                send_sem=halo_send.at[phase, group, by - 1],
                recv_sem=halo_recv.at[phase, group, by - 1],
                device_id=along(by * way),
                device_id_type=MESH,
            )
            for by in (1, 2)
        ]

    def share(phase, group):
        rows = pl.ds(0, CHUNK if phase == 0 else 2 * TOK)
        side = core if group == 0 else 1 - core
        return [
            pltpu.make_async_remote_copy(
                src_ref=held.at[phase, group, 2 * j + 2 * side, :, rows],
                dst_ref=held.at[phase, group, 2 * j + 1, :, rows],
                send_sem=sib_send.at[phase, group, j],
                recv_sem=sib_recv.at[phase, group, j],
                device_id=sibling,
                device_id_type=MESH,
            )
            for j in range(2)
        ]

    targets = ((query_grad, out), (key_grad, value_grad))

    def give(phase, group):
        column = pl.ds(pl.multiple_of((2 * me + phase) * DH, DH), DH)
        copies = []
        for by in (2, 1, 3):
            for a in range(2):
                copies.append(
                    pltpu.make_async_remote_copy(
                        src_ref=result.at[phase, group, a, planes[by]],
                        dst_ref=targets[group][a].at[:, column],
                        send_sem=out_send.at[phase, group, a, by - 1],
                        recv_sem=out_recv.at[phase, group, a, by - 1],
                        device_id=(grp, blk, planes[by]),
                        device_id_type=MESH,
                    )
                )
        own = [
            pltpu.make_async_copy(
                result.at[phase, group, a, me],
                targets[group][a].at[:, column],
                own_sem.at[phase, group, a],
            )
            for a in range(2)
        ]
        return copies, own

    score_scale = 1.0 / math.sqrt(DH)
    norm = 1.0 / math.sqrt(REACH * BLOCK)
    part = ROWS // TOK

    def unit(phase, group, slot, step, diagonal):
        mine = held.at[phase, 1 - group, 0, pl.ds(step * part, part)]
        theirs = held.at[phase, group, slot]
        first = mine[:, 0:TOK, :].reshape(ROWS, DH)
        second = mine[:, TOK : 2 * TOK, :].reshape(ROWS, DH)
        other_first = theirs[:, 0:TOK, :].reshape(BLOCK, DH)
        other_second = theirs[:, TOK : 2 * TOK, :].reshape(BLOCK, DH)
        their_seg = held[0, group, slot, :, 2 * TOK :, :].astype(jnp.float32)
        at = pl.ds(pl.multiple_of(step * ROWS, ROWS), ROWS)
        my_seg = seg_rows[at, :]
        scores = lax.dot_general(first, other_first, NT, preferred_element_type=jnp.float32)
        dprob = lax.dot_general(second, other_second, NT, preferred_element_type=jnp.float32)
        weights, dscores = [], []
        for p in range(PLANES):
            cols = slice(p * TOK, (p + 1) * TOK)
            allowed = my_seg == their_seg[p, 0:1, :]
            if diagonal:
                row = lax.broadcasted_iota(jnp.int32, (ROWS, TOK), 0) + step * ROWS
                col = lax.broadcasted_iota(jnp.int32, (ROWS, TOK), 1) + p * TOK
                allowed = allowed & ((col <= row) if group == 0 else (row <= col))
            v = scores[:, cols] * score_scale
            s = 1.0 / (1.0 + jnp.exp(-v))
            active = v * s
            slope = s + active * (1.0 - s)
            weights.append(jnp.where(allowed, active * norm, 0.0).astype(jnp.bfloat16))
            dscores.append(
                jnp.where(allowed, dprob[:, cols] * slope * (norm * score_scale), 0.0).astype(
                    jnp.bfloat16
                )
            )
        weight = jnp.concatenate(weights, axis=1)
        dscore = jnp.concatenate(dscores, axis=1)
        first_term = lax.dot_general(dscore, other_first, NN, preferred_element_type=jnp.float32)
        second_term = lax.dot_general(weight, other_second, NN, preferred_element_type=jnp.float32)
        if diagonal:
            acc[group, 0, at, :] = first_term
            acc[group, 1, at, :] = second_term
        else:
            acc[group, 0, at, :] += first_term
            acc[group, 1, at, :] += second_term

    steps = BLOCK // ROWS

    def diagonal(phase, group):
        def body(step, carry):
            unit(phase, group, 0, step, True)
            return carry

        lax.fori_loop(0, steps, body, 0)

    def others(phase, group):
        def body(i, carry):
            unit(phase, group, 1 + i // steps, lax.rem(i, steps), False)
            return carry

        lax.fori_loop(0, REACH * steps, body, 0)

    def finish(phase, group):
        for a in range(2):
            for p in range(PLANES):
                result[phase, group, a, p] = acc[group, a, p * TOK : (p + 1) * TOK, :].astype(
                    jnp.bfloat16
                )

    sent = []
    exchanges = {pg: exchange(*pg) for pg in groups}
    halos = {pg: halo(*pg) for pg in groups}
    shares = {pg: share(*pg) for pg in groups}
    gives = {pg: give(*pg) for pg in groups}

    def start_exchange(pg):
        for copy in loads[pg]:
            copy.wait()
        for copy in exchanges[pg]:
            copy.start()

    def arrive(pg):
        for copy in exchanges[pg]:
            copy.wait_recv()

    def start_halo(pg):
        for copy in halos[pg]:
            copy.start()

    def finish_halo(pg):
        for halo_copy, share_copy in zip(halos[pg], shares[pg]):
            halo_copy.wait_recv()
            share_copy.start()
        for share_copy in shares[pg]:
            share_copy.wait_recv()

    def start_give(pg):
        remote, own = gives[pg]
        for copy in remote + own:
            copy.start()

    kv_a, qd_a, kv_b, qd_b = groups
    start_exchange(kv_a)
    start_exchange(qd_a)

    arrive(kv_a)
    start_halo(kv_a)
    start_exchange(kv_b)
    for p in range(PLANES):
        row = held[0, 0, 0, p, 2 * TOK :, :].astype(jnp.float32)[0:1, :]
        seg_rows[p * TOK : (p + 1) * TOK, :] = jnp.broadcast_to(row, (TOK, TOK)).T
        held[0, 1, 0, p, 2 * TOK :, :] = held[0, 0, 0, p, 2 * TOK :, :]

    arrive(qd_a)
    start_halo(qd_a)
    start_exchange(qd_b)
    diagonal(0, 0)
    finish_halo(kv_a)
    others(0, 0)
    finish(0, 0)
    start_give(kv_a)

    arrive(kv_b)
    start_halo(kv_b)
    diagonal(0, 1)
    finish_halo(qd_a)
    others(0, 1)
    finish(0, 1)
    start_give(qd_a)

    arrive(qd_b)
    start_halo(qd_b)
    diagonal(1, 0)
    finish_halo(kv_b)
    others(1, 0)
    finish(1, 0)
    start_give(kv_b)

    diagonal(1, 1)
    finish_halo(qd_b)
    others(1, 1)
    finish(1, 1)
    start_give(qd_b)

    for pg in groups:
        for copy in exchanges[pg] + halos[pg] + shares[pg]:
            copy.wait_send()
    for pg in groups:
        remote, own = gives[pg]
        for copy in remote:
            copy.wait()
        for copy in own:
            copy.wait()


def shards(sizes, queries, keys, values, out_grad, segment):
    tokens, features = queries.shape
    shape = jax.ShapeDtypeStruct((tokens, features), jnp.bfloat16)
    anywhere = pl.BlockSpec(memory_space=pl.ANY)
    dma = pltpu.SemaphoreType.DMA
    return pl.pallas_call(
        functools.partial(kernel, sizes),
        out_shape=(shape,) * 4,
        in_specs=[anywhere] * 4 + [pl.BlockSpec(memory_space=pltpu.VMEM)],
        out_specs=[anywhere] * 4,
        scratch_shapes=[
            pltpu.VMEM((2, 2, REACH + 1, PLANES, CHUNK, DH), jnp.bfloat16),
            pltpu.VMEM((2, 2, PLANES - 1, CHUNK, DH), jnp.bfloat16),
            pltpu.VMEM((2, 2, 2, PLANES, TOK, DH), jnp.bfloat16),
            pltpu.VMEM((2, 2, BLOCK, DH), jnp.float32),
            pltpu.VMEM((BLOCK, TOK), jnp.float32),
            dma((2, 2, PLANES, 2)),
            dma((2, 2, 3)),
            dma((2, 2, 3)),
            dma((2, 2, 2)),
            dma((2, 2, 2)),
            dma((2, 2, 2)),
            dma((2, 2, 2)),
            dma((2, 2, 2, 3)),
            dma((2, 2, 2, 3)),
            dma((2, 2, 2)),
        ],
        compiler_params=pltpu.CompilerParams(
            collective_id=0, has_side_effects=True, vmem_limit_bytes=48 << 20
        ),
        cost_estimate=pl.CostEstimate(
            flops=2 * 2 * 10 * 4 * BLOCK * BLOCK * DH,
            bytes_accessed=8 * tokens * features * 2,
            transcendentals=2 * 10 * BLOCK * BLOCK,
        ),
    )(queries, keys, values, out_grad, segment.reshape(1, tokens))


def solution(mesh):
    rows = P(("grp", "blk", "head"), None)
    return jax.shard_map(
        functools.partial(shards, (mesh.shape["grp"], mesh.shape["blk"])),
        mesh=mesh,
        in_specs=(rows, rows, rows, rows, P(("grp", "blk", "head"))),
        out_specs=(rows,) * 4,
        check_vma=False,
    )
```

```python
import functools
import math

import jax
import jax.numpy as jnp
from jax import lax
from jax.experimental import pallas as pl
from jax.experimental.pallas import tpu as pltpu
from jax.sharding import PartitionSpec as P

MESH = pl.DeviceIdType.MESH
DH = 128
REACH = 4
TOK = 128
PLANES = 4
BLOCK = TOK * PLANES
CHUNK = 2 * TOK + 16
ROWS = 256
NT = (((1,), (1,)), ((), ()))
NN = (((1,), (0,)), ((), ()))


SIDE = 4
CHIPS = SIDE * SIDE


def kernel(
    grps,
    queries, keys, values, out_grad, segment,
    out, query_grad, key_grad, value_grad,
    held, stage, result, acc, seg_rows,
    load_sem, in_send, in_recv, halo_send, halo_recv, sib_send, sib_recv, out_send, out_recv, own_sem,
    relay, piece_send, relay_recv, relay_send, next_send, seg_sem, seg_here,
):
    grp, blk, me = lax.axis_index("grp"), lax.axis_index("blk"), lax.axis_index("head")
    core = lax.rem(blk, 2)
    sibling = (grp, blk + 1 - 2 * core, me)
    planes = [lax.rem(me + by, PLANES) for by in range(PLANES)]

    def mirrored(group, place):
        g, x, y = place
        return place if group else (grps - 1 - g, SIDE - 1 - x, SIDE - 1 - y)

    def device(group, place):
        g, x, y = mirrored(group, place)
        return (g, (x * SIDE + y) * 2 + core, me)

    here = (grp, blk // (2 * SIDE), lax.rem(blk // 2, SIDE))

    def chip(group):
        g, x, y = mirrored(group, here)
        return g, x, y, x * SIDE + y

    def chip_place(g, k):
        return g, k // SIDE, lax.rem(k, SIDE)

    last = (SIDE - 1, SIDE - 1)

    sources = ((keys, values), (queries, out_grad))
    groups = ((0, 0), (0, 1), (1, 0), (1, 1))

    def load(phase, group):
        copies = []
        for by in range(PLANES):
            plane = planes[by]
            column = pl.ds(pl.multiple_of((2 * plane + phase) * DH, DH), DH)
            for a in range(2):
                if by == 0:
                    to = held.at[phase, group, 0, me, pl.ds(a * TOK, TOK)]
                else:
                    to = stage.at[phase, group, by - 1, pl.ds(a * TOK, TOK)]
                copies.append(
                    pltpu.make_async_copy(
                        sources[group][a].at[:, column], to, load_sem.at[phase, group, by, a]
                    )
                )
        return copies

    loads = {pg: load(*pg) for pg in groups}
    for pg in groups:
        for copy in loads[pg]:
            copy.start()

    seg_load = pltpu.make_async_copy(segment, seg_here, seg_sem)
    seg_load.start()

    barrier = pltpu.get_barrier_semaphore()

    def greet(to):
        pl.semaphore_signal(barrier, inc=1, device_id=to, device_id_type=MESH)

    for by in range(1, PLANES):
        greet((grp, blk, planes[by]))
    greet(sibling)
    greeted = PLANES

    def greet_if(condition, partners):
        @pl.when(condition)
        def _():
            for partner in partners:
                greet(partner)

        return jnp.where(condition, len(partners), 0)

    for group in range(2):
        g, x, y, k = chip(group)
        for by in (1, 2):
            greeted += greet_if(k >= by, [device(group, chip_place(g, k - by))])
            greeted += greet_if(k < CHIPS - by, [device(group, chip_place(g, k + by))])
        relays = (y <= 1) & (g >= 1)
        greeted += greet_if(
            relays & (x == 0), [device(group, (g, p, y)) for p in range(1, SIDE)]
        )
        greeted += greet_if(relays & (x > 0), [device(group, (g, 0, y))])
        greeted += greet_if(relays, [device(group, (g - 1, *last))])
        greeted += greet_if(
            (k == CHIPS - 1) & (g < grps - 1),
            [device(group, (g + 1, p, row)) for p in range(SIDE) for row in range(2)],
        )

    def blank(group, slot):
        for phase in range(2):
            held[phase, group, slot, :, 0 : 2 * TOK, :] = jnp.zeros(
                (PLANES, 2 * TOK, DH), jnp.bfloat16
            )
        held[0, group, slot, :, 2 * TOK :, :] = jnp.full((PLANES, 16, DH), -1, jnp.bfloat16)

    def comes(group, by):
        g, x, y, k = chip(group)
        return (g < grps - 1) | (k < CHIPS - by)

    for group in range(2):
        for by in (1, 2):
            pl.when(~comes(group, by))(functools.partial(blank, group, 2 * by))

    seg_load.wait()
    seg = jnp.broadcast_to(seg_here[...].astype(jnp.float32), (16, TOK)).astype(jnp.bfloat16)
    for by in range(3):
        stage[0, 0, by, 2 * TOK :, :] = seg
    held[0, 0, 0, me, 2 * TOK :, :] = seg

    pl.semaphore_wait(barrier, greeted)

    def rows_sent(phase, group):
        return CHUNK if (phase, group) == (0, 0) else 2 * TOK

    def exchange(phase, group):
        rows = pl.ds(0, rows_sent(phase, group))
        return [
            pltpu.make_async_remote_copy(
                src_ref=stage.at[phase, group, by - 1, rows],
                dst_ref=held.at[phase, group, 0, me, rows],
                send_sem=in_send.at[phase, group, by - 1],
                recv_sem=in_recv.at[phase, group, by - 1],
                device_id=(grp, blk, planes[by]),
                device_id_type=MESH,
            )
            for by in (2, 1, 3)
        ]

    def block_rows(phase):
        return pl.ds(0, CHUNK if phase == 0 else 2 * TOK)

    def send(source, to, send_sem, recv_sem, device_id):
        return pltpu.make_async_remote_copy(
            src_ref=source,
            dst_ref=to,
            send_sem=send_sem,
            recv_sem=recv_sem,
            device_id=device_id,
            device_id_type=MESH,
        )

    def halo(phase, group):
        rows = block_rows(phase)
        g, x, y, k = chip(group)
        copies = []
        for by in (1, 2):
            copies.append((
                k >= by,
                send(
                    held.at[phase, group, 0, :, rows],
                    held.at[phase, group, 2 * by, :, rows],
                    halo_send.at[phase, group, by - 1],
                    halo_recv.at[phase, group, by - 1],
                    device(group, chip_place(g, jnp.maximum(k - by, 0))),
                ),
            ))
        edge = (k <= 1) & (g >= 1)
        near_row = jnp.minimum(y, 1)
        for p in range(1, SIDE):
            copies.append((
                edge,
                send(
                    held.at[phase, group, 0, p, rows],
                    relay.at[phase, group, rows],
                    piece_send.at[phase, group, p],
                    relay_recv.at[phase, group],
                    device(group, (g, p, y)),
                ),
            ))
        copies.append((
            edge,
            send(
                held.at[phase, group, 0, 0, rows],
                held.at[phase, group, 2 * (near_row + 1), 0, rows],
                piece_send.at[phase, group, 0],
                halo_recv.at[phase, group, near_row],
                device(group, (jnp.maximum(g - 1, 0), *last)),
            ),
        ))
        return copies

    def pass_piece(phase, group):
        rows = block_rows(phase)
        g, x, y, k = chip(group)
        near_row = jnp.minimum(y, 1)
        return (x >= 1) & (y <= 1) & (g >= 1), send(
            relay.at[phase, group, rows],
            held.at[phase, group, 2 * (near_row + 1), x, rows],
            relay_send.at[phase, group],
            halo_recv.at[phase, group, near_row],
            device(group, (jnp.maximum(g - 1, 0), *last)),
        )

    def pass_block(phase, group):
        rows = block_rows(phase)
        g, x, y, k = chip(group)
        return (k == CHIPS - 1) & (g < grps - 1), send(
            held.at[phase, group, 2, :, rows],
            held.at[phase, group, 4, :, rows],
            next_send.at[phase, group],
            halo_recv.at[phase, group, 1],
            device(group, (g, SIDE - 1, SIDE - 2)),
        )

    def share(phase, group):
        rows = block_rows(phase)
        side = core if group == 0 else 1 - core
        return [
            pltpu.make_async_remote_copy(
                src_ref=held.at[phase, group, 2 * j + 2 * side, :, rows],
                dst_ref=held.at[phase, group, 2 * j + 1, :, rows],
                send_sem=sib_send.at[phase, group, j],
                recv_sem=sib_recv.at[phase, group, j],
                device_id=sibling,
                device_id_type=MESH,
            )
            for j in range(2)
        ]

    targets = ((query_grad, out), (key_grad, value_grad))

    def give(phase, group):
        column = pl.ds(pl.multiple_of((2 * me + phase) * DH, DH), DH)
        copies = []
        for by in (2, 1, 3):
            for a in range(2):
                copies.append(
                    pltpu.make_async_remote_copy(
                        src_ref=result.at[phase, group, a, planes[by]],
                        dst_ref=targets[group][a].at[:, column],
                        send_sem=out_send.at[phase, group, a, by - 1],
                        recv_sem=out_recv.at[phase, group, a, by - 1],
                        device_id=(grp, blk, planes[by]),
                        device_id_type=MESH,
                    )
                )
        own = [
            pltpu.make_async_copy(
                result.at[phase, group, a, me],
                targets[group][a].at[:, column],
                own_sem.at[phase, group, a],
            )
            for a in range(2)
        ]
        return copies, own

    score_scale = 1.0 / math.sqrt(DH)
    norm = 1.0 / math.sqrt(REACH * BLOCK)
    part = ROWS // TOK

    def unit(phase, group, slot, step, diagonal):
        mine = held.at[phase, 1 - group, 0, pl.ds(step * part, part)]
        theirs = held.at[phase, group, slot]
        first = mine[:, 0:TOK, :].reshape(ROWS, DH)
        second = mine[:, TOK : 2 * TOK, :].reshape(ROWS, DH)
        other_first = theirs[:, 0:TOK, :].reshape(BLOCK, DH)
        other_second = theirs[:, TOK : 2 * TOK, :].reshape(BLOCK, DH)
        their_seg = held[0, group, slot, :, 2 * TOK :, :].astype(jnp.float32)
        at = pl.ds(pl.multiple_of(step * ROWS, ROWS), ROWS)
        my_seg = seg_rows[at, :]
        scores = lax.dot_general(first, other_first, NT, preferred_element_type=jnp.float32)
        dprob = lax.dot_general(second, other_second, NT, preferred_element_type=jnp.float32)
        weights, dscores = [], []
        for p in range(PLANES):
            cols = slice(p * TOK, (p + 1) * TOK)
            allowed = my_seg == their_seg[p, 0:1, :]
            if diagonal:
                row = lax.broadcasted_iota(jnp.int32, (ROWS, TOK), 0) + step * ROWS
                col = lax.broadcasted_iota(jnp.int32, (ROWS, TOK), 1) + p * TOK
                allowed = allowed & ((col <= row) if group == 0 else (row <= col))
            v = scores[:, cols] * score_scale
            s = 1.0 / (1.0 + jnp.exp(-v))
            active = v * s
            slope = s + active * (1.0 - s)
            weights.append(jnp.where(allowed, active * norm, 0.0).astype(jnp.bfloat16))
            dscores.append(
                jnp.where(allowed, dprob[:, cols] * slope * (norm * score_scale), 0.0).astype(
                    jnp.bfloat16
                )
            )
        weight = jnp.concatenate(weights, axis=1)
        dscore = jnp.concatenate(dscores, axis=1)
        first_term = lax.dot_general(dscore, other_first, NN, preferred_element_type=jnp.float32)
        second_term = lax.dot_general(weight, other_second, NN, preferred_element_type=jnp.float32)
        if diagonal:
            acc[group, 0, at, :] = first_term
            acc[group, 1, at, :] = second_term
        else:
            acc[group, 0, at, :] += first_term
            acc[group, 1, at, :] += second_term

    steps = BLOCK // ROWS

    def diagonal(phase, group):
        def body(step, carry):
            unit(phase, group, 0, step, True)
            return carry

        lax.fori_loop(0, steps, body, 0)

    def others(phase, group):
        def body(i, carry):
            unit(phase, group, 1 + i // steps, lax.rem(i, steps), False)
            return carry

        lax.fori_loop(0, REACH * steps, body, 0)

    def finish(phase, group):
        for a in range(2):
            for p in range(PLANES):
                result[phase, group, a, p] = acc[group, a, p * TOK : (p + 1) * TOK, :].astype(
                    jnp.bfloat16
                )

    exchanges = {pg: exchange(*pg) for pg in groups}
    halos = {pg: halo(*pg) for pg in groups}
    passed = {pg: pass_piece(*pg) for pg in groups}
    seconds = {pg: pass_block(*pg) for pg in groups}
    shares = {pg: share(*pg) for pg in groups}
    gives = {pg: give(*pg) for pg in groups}

    def start_exchange(pg):
        for copy in loads[pg]:
            copy.wait()
        for copy in exchanges[pg]:
            copy.start()

    def arrive(pg):
        for copy in exchanges[pg]:
            copy.wait_recv()

    def start_halo(pg):
        for condition, copy in halos[pg]:
            pl.when(condition)(copy.start)

    def hand_on(pg):
        condition, copy = passed[pg]

        @pl.when(condition)
        def _():
            pltpu.make_async_copy(copy.src_ref, copy.src_ref, relay_recv.at[pg]).wait()
            copy.start()

    def near(pg):
        pl.when(comes(pg[1], 1))(halos[pg][0][1].wait_recv)
        condition, copy = seconds[pg]
        pl.when(condition)(copy.start)
        shares[pg][0].start()

    def far(pg):
        pl.when(comes(pg[1], 2))(halos[pg][1][1].wait_recv)
        shares[pg][1].start()
        for copy in shares[pg]:
            copy.wait_recv()

    def start_give(pg):
        finish(*pg)
        remote, own = gives[pg]
        for copy in remote + own:
            copy.start()

    kv_a, qd_a, kv_b, qd_b = groups
    start_exchange(kv_a)
    start_exchange(qd_a)

    arrive(kv_a)
    start_halo(kv_a)
    start_exchange(kv_b)
    for p in range(PLANES):
        row = held[0, 0, 0, p, 2 * TOK :, :].astype(jnp.float32)[0:1, :]
        seg_rows[p * TOK : (p + 1) * TOK, :] = jnp.broadcast_to(row, (TOK, TOK)).T
        held[0, 1, 0, p, 2 * TOK :, :] = held[0, 0, 0, p, 2 * TOK :, :]
    hand_on(kv_a)
    near(kv_a)

    arrive(qd_a)
    start_halo(qd_a)
    start_exchange(qd_b)
    diagonal(*kv_a)
    far(kv_a)
    hand_on(qd_a)
    others(*kv_a)
    start_give(kv_a)
    near(qd_a)
    diagonal(*qd_a)
    far(qd_a)
    others(*qd_a)
    start_give(qd_a)

    arrive(kv_b)
    start_halo(kv_b)
    hand_on(kv_b)
    near(kv_b)
    arrive(qd_b)
    start_halo(qd_b)
    diagonal(*kv_b)
    far(kv_b)
    hand_on(qd_b)
    others(*kv_b)
    start_give(kv_b)
    near(qd_b)
    diagonal(*qd_b)
    far(qd_b)
    others(*qd_b)
    start_give(qd_b)

    for pg in groups:
        for copy in exchanges[pg] + shares[pg]:
            copy.wait_send()
        for condition, copy in halos[pg] + [passed[pg], seconds[pg]]:
            pl.when(condition)(copy.wait_send)
    for pg in groups:
        remote, own = gives[pg]
        for copy in remote + own:
            copy.wait()


def hand_over(*refs):
    copies = [
        pltpu.make_async_copy(refs[i], refs[4 + i], refs[8].at[i]) for i in range(4)
    ]
    for copy in copies:
        copy.start()
    for copy in copies:
        copy.wait()


def shards(grps, queries, keys, values, out_grad, segment):
    tokens, features = queries.shape
    shape = jax.ShapeDtypeStruct((tokens, features), jnp.bfloat16)
    anywhere = pl.BlockSpec(memory_space=pl.ANY)
    dma = pltpu.SemaphoreType.DMA
    results = pl.pallas_call(
        functools.partial(kernel, grps),
        out_shape=(shape,) * 4,
        in_specs=[anywhere] * 5,
        out_specs=[anywhere] * 4,
        scratch_shapes=[
            pltpu.VMEM((2, 2, REACH + 1, PLANES, CHUNK, DH), jnp.bfloat16),
            pltpu.VMEM((2, 2, PLANES - 1, CHUNK, DH), jnp.bfloat16),
            pltpu.VMEM((2, 2, 2, PLANES, TOK, DH), jnp.bfloat16),
            pltpu.VMEM((2, 2, BLOCK, DH), jnp.float32),
            pltpu.VMEM((BLOCK, TOK), jnp.float32),
            dma((2, 2, PLANES, 2)),
            dma((2, 2, 3)),
            dma((2, 2, 3)),
            dma((2, 2, 2)),
            dma((2, 2, 2)),
            dma((2, 2, 2)),
            dma((2, 2, 2)),
            dma((2, 2, 2, 3)),
            dma((2, 2, 2, 3)),
            dma((2, 2, 2)),
            pltpu.VMEM((2, 2, CHUNK, DH), jnp.bfloat16),
            dma((2, 2, SIDE)),
            dma((2, 2)),
            dma((2, 2)),
            dma((2, 2)),
            dma(()),
            pltpu.VMEM((1, TOK), jnp.int32),
        ],
        compiler_params=pltpu.CompilerParams(
            collective_id=0, has_side_effects=True, vmem_limit_bytes=60 << 20
        ),
        cost_estimate=pl.CostEstimate(
            flops=2 * 2 * 10 * 4 * BLOCK * BLOCK * DH,
            bytes_accessed=8 * tokens * features * 2,
            transcendentals=2 * 10 * BLOCK * BLOCK,
        ),
    )(queries, keys, values, out_grad, segment.reshape(1, tokens))
    return pl.pallas_call(
        hand_over,
        out_shape=(shape,) * 4,
        in_specs=[anywhere] * 4,
        out_specs=[anywhere] * 4,
        scratch_shapes=[dma((4,))],
        compiler_params=pltpu.CompilerParams(vmem_limit_bytes=60 << 20),
    )(*results)


def solution(mesh):
    rows = P(("grp", "blk", "head"), None)
    return jax.shard_map(
        functools.partial(shards, mesh.shape["grp"]),
        mesh=mesh,
        in_specs=(rows, rows, rows, rows, P(("grp", "blk", "head"))),
        out_specs=(rows,) * 4,
        check_vma=False,
    )
```

```python
import functools
import math

import jax
import jax.numpy as jnp
from jax import lax
from jax.experimental import pallas as pl
from jax.experimental.pallas import tpu as pltpu
from jax.sharding import PartitionSpec as P

MESH = pl.DeviceIdType.MESH
LOG2E = math.log2(math.e)
DH = 128
REACH = 4
TOK = 128
PLANES = 4
BLOCK = TOK * PLANES
CHUNK = 2 * TOK + 16
PART = 64
PARTS = 2 * TOK // PART
ROWS = 512
NT = (((1,), (1,)), ((), ()))
NN = (((1,), (0,)), ((), ()))


SIDE = 4
CHIPS = SIDE * SIDE


def kernel(
    grps,
    queries, keys, values, out_grad, segment,
    out, query_grad, key_grad, value_grad,
    held, stage, result, acc, seg_rows,
    load_sem, in_send, in_recv, halo_send, halo_recv, sib_send, sib_recv, out_send, out_recv, own_sem,
    relay, piece_send, relay_recv, relay_send, next_send, seg_sem, seg_here,
):
    grp, blk, me = lax.axis_index("grp"), lax.axis_index("blk"), lax.axis_index("head")
    core = lax.rem(blk, 2)
    sibling = (grp, blk + 1 - 2 * core, me)
    planes = [lax.rem(me + by, PLANES) for by in range(PLANES)]

    def mirrored(group, place):
        turned = [n - 1 - at for n, at in zip((grps, SIDE, SIDE), place)]
        if isinstance(group, int):
            return tuple(place if group else turned)
        return tuple(jnp.where(group == 1, *pair) for pair in zip(place, turned))

    def device(group, place):
        g, x, y = mirrored(group, place)
        return (g, (x * SIDE + y) * 2 + core, me)

    here = (grp, blk // (2 * SIDE), lax.rem(blk // 2, SIDE))

    def chip(group):
        g, x, y = mirrored(group, here)
        return g, x, y, x * SIDE + y

    def chip_place(g, k):
        return g, k // SIDE, lax.rem(k, SIDE)

    last = (SIDE - 1, SIDE - 1)

    first = jnp.where(chip(1)[3] <= 1, 1, 0)
    order = (first, 1 - first)

    sources = ((keys, values), (queries, out_grad))
    groups = ((0, 0), (0, 1), (1, 0), (1, 1))

    def load(phase, group):
        copies = []
        for by in range(PLANES):
            plane = planes[by]
            column = pl.ds(pl.multiple_of((2 * plane + phase) * DH, DH), DH)
            for a in range(2):
                if by == 0:
                    to = held.at[phase, group, 0, me, pl.ds(a * TOK, TOK)]
                else:
                    to = stage.at[phase, group, by - 1, pl.ds(a * TOK, TOK)]
                copies.append(
                    pltpu.make_async_copy(
                        sources[group][a].at[:, column], to, load_sem.at[phase, group, by, a]
                    )
                )
        return copies

    loads = {pg: load(*pg) for pg in groups}
    for pg in groups:
        for copy in loads[pg]:
            copy.start()

    seg_load = pltpu.make_async_copy(segment, seg_here, seg_sem)
    seg_load.start()

    barrier = pltpu.get_barrier_semaphore()

    def greet(to):
        pl.semaphore_signal(barrier, inc=1, device_id=to, device_id_type=MESH)

    for by in range(1, PLANES):
        greet((grp, blk, planes[by]))
    greet(sibling)
    greeted = PLANES

    def greet_if(condition, partners):
        @pl.when(condition)
        def _():
            for partner in partners:
                greet(partner)

        return jnp.where(condition, len(partners), 0)

    for group in range(2):
        g, x, y, k = chip(group)
        for by in (1, 2):
            greeted += greet_if(k >= by, [device(group, chip_place(g, k - by))])
            greeted += greet_if(k < CHIPS - by, [device(group, chip_place(g, k + by))])
        relays = (y <= 1) & (g >= 1)
        greeted += greet_if(
            relays & (x == 0), [device(group, (g, p, y)) for p in range(1, SIDE)]
        )
        greeted += greet_if(relays & (x > 0), [device(group, (g, 0, y))])
        greeted += greet_if(relays, [device(group, (g - 1, *last))])
        greeted += greet_if(
            (k == CHIPS - 1) & (g < grps - 1),
            [device(group, (g + 1, p, row)) for p in range(SIDE) for row in range(2)],
        )

    def blank(group, slot):
        for phase in range(2):
            held[phase, group, slot, :, 0 : 2 * TOK, :] = jnp.zeros(
                (PLANES, 2 * TOK, DH), jnp.bfloat16
            )
        held[0, group, slot, :, 2 * TOK :, :] = jnp.full((PLANES, 16, DH), -1, jnp.bfloat16)

    def comes(group, by):
        g, x, y, k = chip(group)
        return (g < grps - 1) | (k < CHIPS - by)

    for group in range(2):
        for by in (1, 2):
            pl.when(~comes(group, by))(functools.partial(blank, group, 2 * by))

    seg_load.wait()
    seg = jnp.broadcast_to(seg_here[...].astype(jnp.float32), (16, TOK)).astype(jnp.bfloat16)
    for group in range(2):
        for by in range(3):
            stage[0, group, by, 2 * TOK :, :] = seg
        held[0, group, 0, me, 2 * TOK :, :] = seg

    pl.semaphore_wait(barrier, greeted)

    def exchange(phase, turn):
        group = order[turn]
        total = CHUNK if phase == turn == 0 else 2 * TOK
        parts = []
        for n in range(PARTS):
            rows = pl.ds(n * PART, total - n * PART if n == PARTS - 1 else PART)
            parts.append([
                pltpu.make_async_remote_copy(
                    src_ref=stage.at[phase, group, by - 1, rows],
                    dst_ref=held.at[phase, group, 0, me, rows],
                    send_sem=in_send.at[phase, group, n, by - 1],
                    recv_sem=in_recv.at[phase, group, n, by - 1],
                    device_id=(grp, blk, planes[by]),
                    device_id_type=MESH,
                )
                for by in (2, 1, 3)
            ])
        return parts

    def block_rows(phase):
        return pl.ds(0, CHUNK if phase == 0 else 2 * TOK)

    def send(source, to, send_sem, recv_sem, device_id):
        return pltpu.make_async_remote_copy(
            src_ref=source,
            dst_ref=to,
            send_sem=send_sem,
            recv_sem=recv_sem,
            device_id=device_id,
            device_id_type=MESH,
        )

    def halo(phase, group):
        rows = block_rows(phase)
        g, x, y, k = chip(group)
        copies = []
        for by in (1, 2):
            copies.append((
                k >= by,
                send(
                    held.at[phase, group, 0, :, rows],
                    held.at[phase, group, 2 * by, :, rows],
                    halo_send.at[phase, group, by - 1],
                    halo_recv.at[phase, group, by - 1],
                    device(group, chip_place(g, jnp.maximum(k - by, 0))),
                ),
            ))
        edge = (k <= 1) & (g >= 1)
        near_row = jnp.minimum(y, 1)
        for p in range(1, SIDE):
            copies.append((
                edge,
                send(
                    held.at[phase, group, 0, p, rows],
                    relay.at[phase, group, rows],
                    piece_send.at[phase, group, p],
                    relay_recv.at[phase, group],
                    device(group, (g, p, y)),
                ),
            ))
        copies.append((
            edge,
            send(
                held.at[phase, group, 0, 0, rows],
                held.at[phase, group, 2 * (near_row + 1), 0, rows],
                piece_send.at[phase, group, 0],
                halo_recv.at[phase, group, near_row],
                device(group, (jnp.maximum(g - 1, 0), *last)),
            ),
        ))
        return copies

    def pass_piece(phase, group):
        rows = block_rows(phase)
        g, x, y, k = chip(group)
        near_row = jnp.minimum(y, 1)
        return (x >= 1) & (y <= 1) & (g >= 1), send(
            relay.at[phase, group, rows],
            held.at[phase, group, 2 * (near_row + 1), x, rows],
            relay_send.at[phase, group],
            halo_recv.at[phase, group, near_row],
            device(group, (jnp.maximum(g - 1, 0), *last)),
        )

    def pass_block(phase, group):
        rows = block_rows(phase)
        g, x, y, k = chip(group)
        return (k == CHIPS - 1) & (g < grps - 1), send(
            held.at[phase, group, 2, :, rows],
            held.at[phase, group, 4, :, rows],
            next_send.at[phase, group],
            halo_recv.at[phase, group, 1],
            device(group, (g, SIDE - 1, SIDE - 2)),
        )

    def share(phase, group):
        rows = block_rows(phase)
        side = core if group == 0 else 1 - core
        return [
            pltpu.make_async_remote_copy(
                src_ref=held.at[phase, group, 2 * j + 2 * side, :, rows],
                dst_ref=held.at[phase, group, 2 * j + 1, :, rows],
                send_sem=sib_send.at[phase, group, j],
                recv_sem=sib_recv.at[phase, group, j],
                device_id=sibling,
                device_id_type=MESH,
            )
            for j in range(2)
        ]

    targets = ((query_grad, out), (key_grad, value_grad))

    def give(phase, group):
        column = pl.ds(pl.multiple_of((2 * me + phase) * DH, DH), DH)
        parts = []
        for n in range(PARTS):
            a, rows = n * PART // TOK, pl.ds(n * PART % TOK, PART)
            parts.append([
                pltpu.make_async_remote_copy(
                    src_ref=result.at[phase, group, a, planes[by], rows],
                    dst_ref=targets[group][a].at[rows, column],
                    send_sem=out_send.at[phase, group, n, by - 1],
                    recv_sem=out_recv.at[phase, group, n, by - 1],
                    device_id=(grp, blk, planes[by]),
                    device_id_type=MESH,
                )
                for by in (2, 1, 3)
            ])
        own = [
            pltpu.make_async_copy(
                result.at[phase, group, a, me],
                targets[group][a].at[:, column],
                own_sem.at[phase, group, a],
            )
            for a in range(2)
        ]
        return parts, own

    score_scale = 1.0 / math.sqrt(DH)
    both_scales = 1.0 / math.sqrt(DH * REACH * BLOCK)
    part = ROWS // TOK

    def unit(phase, group, slot, step, diagonal):
        mine = held.at[phase, 1 - group, 0, pl.ds(step * part, part)]
        theirs = held.at[phase, group, slot]
        first = mine[:, 0:TOK, :].reshape(ROWS, DH)
        second = mine[:, TOK : 2 * TOK, :].reshape(ROWS, DH)
        other_first = theirs[:, 0:TOK, :].reshape(BLOCK, DH)
        other_second = theirs[:, TOK : 2 * TOK, :].reshape(BLOCK, DH)
        their_seg = held[0, group, slot, :, 2 * TOK :, :].astype(jnp.float32)
        at = pl.ds(pl.multiple_of(step * ROWS, ROWS), ROWS)
        my_seg = seg_rows[at, :]
        scores = lax.dot_general(first, other_first, NT, preferred_element_type=jnp.float32)
        dprob = lax.dot_general(second, other_second, NT, preferred_element_type=jnp.float32)
        weights, dscores = [], []
        for p in range(PLANES):
            cols = slice(p * TOK, (p + 1) * TOK)
            allowed = my_seg == their_seg[p, 0:1, :]
            if diagonal:
                row = lax.broadcasted_iota(jnp.int32, (ROWS, TOK), 0) + step * ROWS
                col = lax.broadcasted_iota(jnp.int32, (ROWS, TOK), 1) + p * TOK
                allowed = allowed & ((col <= row) if group == 0 else (row <= col))
            raw = scores[:, cols]
            grown = 1.0 + jnp.exp2(jnp.minimum(raw * (-score_scale * LOG2E), 115.0))
            s = pl.reciprocal(grown, approx=True)
            s = s * (2.0 - grown * s)
            active = raw * s
            slope = s + active * (score_scale - score_scale * s)
            weights.append(jnp.where(allowed, active, 0.0).astype(jnp.bfloat16))
            dscores.append(jnp.where(allowed, dprob[:, cols] * slope, 0.0).astype(jnp.bfloat16))
        weight = jnp.concatenate(weights, axis=1)
        dscore = jnp.concatenate(dscores, axis=1)
        first_term = lax.dot_general(dscore, other_first, NN, preferred_element_type=jnp.float32)
        second_term = lax.dot_general(weight, other_second, NN, preferred_element_type=jnp.float32)
        if diagonal:
            acc[group, 0, at, :] = first_term
            acc[group, 1, at, :] = second_term
        else:
            acc[group, 0, at, :] += first_term
            acc[group, 1, at, :] += second_term

    steps = BLOCK // ROWS

    def diagonal(phase, group):
        def body(step, carry):
            unit(phase, group, 0, step, True)
            return carry

        lax.fori_loop(0, steps, body, 0)

    def others(phase, group):
        def body(i, carry):
            unit(phase, group, 1 + i // steps, lax.rem(i, steps), False)
            return carry

        lax.fori_loop(0, REACH * steps, body, 0)

    def finish(phase, group):
        for a in range(2):
            for p in range(PLANES):
                total = acc[group, a, p * TOK : (p + 1) * TOK, :] * both_scales
                result[phase, group, a, p] = total.astype(jnp.bfloat16)

    exchanges = {pg: exchange(*pg) for pg in groups}
    halos = {pg: halo(*pg) for pg in groups}
    passed = {pg: pass_piece(*pg) for pg in groups}
    seconds = {pg: pass_block(*pg) for pg in groups}
    shares = {pg: share(*pg) for pg in groups}
    gives = {pg: give(*pg) for pg in groups}

    queue = [part for pg in groups for part in exchanges[pg]]
    queue += [part for pg in groups for part in gives[pg][0]]
    window = 3
    issued = []
    gone = []

    def left(count):
        for n in range(len(gone), count):
            for copy in queue[n]:
                copy.wait_send()
            gone.append(n)

    def issue(count, limited=True):
        for n in range(len(issued), len(issued) + count):
            if limited:
                left(n - window + 1)
            if n in (0, 2 * PARTS):
                for group in range(2):
                    for copy in loads[n // (2 * PARTS), group]:
                        copy.wait()
            for copy in queue[n]:
                copy.start()
            issued.append(n)

    def arrive(phase, turn):
        for part in exchanges[phase, turn]:
            for copy in part:
                copy.wait_recv()

    def start_halo(phase, turn):
        for condition, copy in halo(phase, order[turn]):
            pl.when(condition)(copy.start)

    def hand_on(pg):
        condition, copy = passed[pg]

        @pl.when(condition)
        def _():
            pltpu.make_async_copy(copy.src_ref, copy.src_ref, relay_recv.at[pg]).wait()
            copy.start()

    def near(pg):
        pl.when(comes(pg[1], 1))(halos[pg][0][1].wait_recv)
        condition, copy = seconds[pg]
        pl.when(condition)(copy.start)
        shares[pg][0].start()

    def far(pg):
        pl.when(comes(pg[1], 2))(halos[pg][1][1].wait_recv)
        shares[pg][1].start()
        for copy in shares[pg]:
            copy.wait_recv()

    def start_give(pg):
        finish(*pg)
        for copy in gives[pg][1]:
            copy.start()

    kv_a, qd_a, kv_b, qd_b = groups
    issue(7)
    arrive(0, 0)
    theirs, mine = held.at[0, order[0], 0], held.at[0, order[1], 0]
    for p in range(PLANES):
        numbers = theirs[p, 2 * TOK :, :]
        mine[p, 2 * TOK :, :] = numbers
        row = numbers.astype(jnp.float32)[0:1, :]
        seg_rows[p * TOK : (p + 1) * TOK, :] = jnp.broadcast_to(row, (TOK, TOK)).T
    start_halo(0, 0)
    issue(1)
    hand_on(kv_a)
    hand_on(qd_a)
    issue(3)

    arrive(0, 1)
    start_halo(0, 1)
    issue(1)
    near(kv_a)
    diagonal(*kv_a)
    issue(1)
    far(kv_a)
    issue(1)
    others(*kv_a)
    start_give(kv_a)
    issue(2)

    arrive(1, 0)
    start_halo(1, 0)
    near(qd_a)
    diagonal(*qd_a)
    hand_on(kv_b)
    hand_on(qd_b)
    issue(1)
    far(qd_a)
    others(*qd_a)
    start_give(qd_a)
    issue(2)

    arrive(1, 1)
    start_halo(1, 1)
    near(kv_b)
    diagonal(*kv_b)
    issue(6 * PARTS - len(issued), limited=False)
    far(kv_b)
    others(*kv_b)
    start_give(kv_b)
    issue(PARTS, limited=False)

    near(qd_b)
    diagonal(*qd_b)
    far(qd_b)
    others(*qd_b)
    start_give(qd_b)
    issue(PARTS, limited=False)

    left(len(queue))
    for pg in groups:
        for copy in shares[pg]:
            copy.wait_send()
        for condition, copy in halos[pg] + [passed[pg], seconds[pg]]:
            pl.when(condition)(copy.wait_send)
    for pg in groups:
        parts, own = gives[pg]
        for part in parts:
            for copy in part:
                copy.wait_recv()
        for copy in own:
            copy.wait()


def hand_over(*refs):
    ins, outs, (here, sems) = refs[:4], refs[4:8], refs[8:]
    arriving = [pltpu.make_async_copy(ins[i], here.at[i], sems.at[0, i]) for i in range(4)]
    leaving = [pltpu.make_async_copy(here.at[i], outs[i], sems.at[1, i]) for i in range(4)]
    for copy in arriving:
        copy.start()
    for i in range(4):
        arriving[i].wait()
        leaving[i].start()
    for copy in leaving:
        copy.wait()


def shards(grps, queries, keys, values, out_grad, segment):
    tokens, features = queries.shape
    shape = jax.ShapeDtypeStruct((tokens, features), jnp.bfloat16)
    anywhere = pl.BlockSpec(memory_space=pl.ANY)
    dma = pltpu.SemaphoreType.DMA
    results = pl.pallas_call(
        functools.partial(kernel, grps),
        out_shape=(shape,) * 4,
        in_specs=[anywhere] * 5,
        out_specs=[anywhere] * 4,
        scratch_shapes=[
            pltpu.VMEM((2, 2, REACH + 1, PLANES, CHUNK, DH), jnp.bfloat16),
            pltpu.VMEM((2, 2, PLANES - 1, CHUNK, DH), jnp.bfloat16),
            pltpu.VMEM((2, 2, 2, PLANES, TOK, DH), jnp.bfloat16),
            pltpu.VMEM((2, 2, BLOCK, DH), jnp.float32),
            pltpu.VMEM((BLOCK, TOK), jnp.float32),
            dma((2, 2, PLANES, 2)),
            dma((2, 2, PARTS, 3)),
            dma((2, 2, PARTS, 3)),
            dma((2, 2, 2)),
            dma((2, 2, 2)),
            dma((2, 2, 2)),
            dma((2, 2, 2)),
            dma((2, 2, PARTS, 3)),
            dma((2, 2, PARTS, 3)),
            dma((2, 2, 2)),
            pltpu.VMEM((2, 2, CHUNK, DH), jnp.bfloat16),
            dma((2, 2, SIDE)),
            dma((2, 2)),
            dma((2, 2)),
            dma((2, 2)),
            dma(()),
            pltpu.VMEM((1, TOK), jnp.int32),
        ],
        compiler_params=pltpu.CompilerParams(
            collective_id=0, has_side_effects=True, vmem_limit_bytes=60 << 20
        ),
        cost_estimate=pl.CostEstimate(
            flops=2 * 2 * 10 * 4 * BLOCK * BLOCK * DH,
            bytes_accessed=8 * tokens * features * 2,
            transcendentals=2 * 10 * BLOCK * BLOCK,
        ),
    )(queries, keys, values, out_grad, segment.reshape(1, tokens))
    return pl.pallas_call(
        hand_over,
        out_shape=(shape,) * 4,
        in_specs=[anywhere] * 4,
        out_specs=[anywhere] * 4,
        scratch_shapes=[pltpu.VMEM((4, tokens, features), jnp.bfloat16), dma((2, 4))],
        compiler_params=pltpu.CompilerParams(vmem_limit_bytes=60 << 20),
    )(*results)


def solution(mesh):
    rows = P(("grp", "blk", "head"), None)
    return jax.shard_map(
        functools.partial(shards, mesh.shape["grp"]),
        mesh=mesh,
        in_specs=(rows, rows, rows, rows, P(("grp", "blk", "head"))),
        out_specs=(rows,) * 4,
        check_vma=False,
    )
```

```python
import functools
import math

import jax
import jax.numpy as jnp
from jax import lax
from jax.experimental import pallas as pl
from jax.experimental.pallas import tpu as pltpu
from jax.sharding import PartitionSpec as P

MESH = pl.DeviceIdType.MESH
LOG2E = math.log2(math.e)
DH = 128
REACH = 4
TOK = 128
PLANES = 4
BLOCK = TOK * PLANES
CHUNK = 2 * TOK + 16
PART = 64
PARTS = 2 * TOK // PART
ROWS = 512
NT = (((1,), (1,)), ((), ()))
NN = (((1,), (0,)), ((), ()))


SIDE = 4
CHIPS = SIDE * SIDE


def kernel(
    grps,
    queries, keys, values, out_grad, segment,
    out, query_grad, key_grad, value_grad,
    held, stage, result, acc, seg_rows,
    load_sem, in_send, in_recv, halo_send, halo_recv, sib_send, sib_recv, out_send, out_recv, own_sem,
    relay, piece_send, relay_recv, relay_send, next_send, seg_sem, seg_here,
):
    grp, blk, me = lax.axis_index("grp"), lax.axis_index("blk"), lax.axis_index("head")
    core = lax.rem(blk, 2)
    sibling = (grp, blk + 1 - 2 * core, me)
    planes = [lax.rem(me + by, PLANES) for by in range(PLANES)]

    def mirrored(group, place):
        turned = [n - 1 - at for n, at in zip((grps, SIDE, SIDE), place)]
        if isinstance(group, int):
            return tuple(place if group else turned)
        return tuple(jnp.where(group == 1, *pair) for pair in zip(place, turned))

    def device(group, place):
        g, x, y = mirrored(group, place)
        return (g, (x * SIDE + y) * 2 + core, me)

    here = (grp, blk // (2 * SIDE), lax.rem(blk // 2, SIDE))

    def chip(group):
        g, x, y = mirrored(group, here)
        return g, x, y, x * SIDE + y

    def chip_place(g, k):
        return g, k // SIDE, lax.rem(k, SIDE)

    last = (SIDE - 1, SIDE - 1)

    first = jnp.where((chip(1)[3] <= 1) & (grp >= 1), 1, 0)
    order = ((0, 1), (first, 1 - first))

    sources = ((keys, values), (queries, out_grad))
    groups = ((0, 0), (0, 1), (1, 0), (1, 1))

    def load(phase, group):
        copies = []
        for by in range(PLANES):
            plane = planes[by]
            column = pl.ds(pl.multiple_of((2 * plane + phase) * DH, DH), DH)
            for a in range(2):
                if by == 0:
                    to = held.at[phase, group, 0, me, pl.ds(a * TOK, TOK)]
                else:
                    to = stage.at[phase, group, by - 1, pl.ds(a * TOK, TOK)]
                copies.append(
                    pltpu.make_async_copy(
                        sources[group][a].at[:, column], to, load_sem.at[phase, group, by, a]
                    )
                )
        return copies

    loads = {pg: load(*pg) for pg in groups}
    for pg in groups:
        for copy in loads[pg]:
            copy.start()

    seg_load = pltpu.make_async_copy(segment, seg_here, seg_sem)
    seg_load.start()

    barrier = pltpu.get_barrier_semaphore()

    def greet(to):
        pl.semaphore_signal(barrier, inc=1, device_id=to, device_id_type=MESH)

    for by in range(1, PLANES):
        greet((grp, blk, planes[by]))
    greet(sibling)
    greeted = PLANES

    def greet_if(condition, partners):
        @pl.when(condition)
        def _():
            for partner in partners:
                greet(partner)

        return jnp.where(condition, len(partners), 0)

    for group in range(2):
        g, x, y, k = chip(group)
        for by in (1, 2):
            greeted += greet_if(k >= by, [device(group, chip_place(g, k - by))])
            greeted += greet_if(k < CHIPS - by, [device(group, chip_place(g, k + by))])
        greeted += greet_if(
            (x == 0) & (y <= 1) & (g >= 1),
            [device(group, (g, p, y)) for p in range(1, SIDE)]
            + [device(group, (g, p, SIDE - 1 - y)) for p in range(SIDE)],
        )
        greeted += greet_if((x > 0) & (y <= 1) & (g >= 1), [device(group, (g, 0, y))])
        greeted += greet_if((y >= 2) & (g >= 1), [device(group, (g, 0, SIDE - 1 - y))])
        greeted += greet_if(g >= 1, [device(group, (g - 1, *last))])
        greeted += greet_if(
            (k == CHIPS - 1) & (g < grps - 1),
            [device(group, (g + 1, p, row)) for p in range(SIDE) for row in range(SIDE)],
        )

    def blank(group, slot):
        for phase in range(2):
            held[phase, group, slot, :, 0 : 2 * TOK, :] = jnp.zeros(
                (PLANES, 2 * TOK, DH), jnp.bfloat16
            )
        held[0, group, slot, :, 2 * TOK :, :] = jnp.full((PLANES, 16, DH), -1, jnp.bfloat16)

    def comes(group, by):
        g, x, y, k = chip(group)
        return (g < grps - 1) | (k < CHIPS - by)

    for group in range(2):
        for by in (1, 2):
            pl.when(~comes(group, by))(functools.partial(blank, group, 2 * by))

    seg_load.wait()
    seg = jnp.broadcast_to(seg_here[...].astype(jnp.float32), (16, TOK)).astype(jnp.bfloat16)
    for by in range(3):
        stage[0, 0, by, 2 * TOK :, :] = seg
    held[0, 0, 0, me, 2 * TOK :, :] = seg

    pl.semaphore_wait(barrier, greeted)

    def exchange(phase, turn):
        group = order[phase][turn]
        total = CHUNK if phase == turn == 0 else 2 * TOK
        parts = []
        for n in range(PARTS):
            rows = pl.ds(n * PART, total - n * PART if n == PARTS - 1 else PART)
            parts.append([
                pltpu.make_async_remote_copy(
                    src_ref=stage.at[phase, group, by - 1, rows],
                    dst_ref=held.at[phase, group, 0, me, rows],
                    send_sem=in_send.at[phase, group, n, by - 1],
                    recv_sem=in_recv.at[phase, group, n, by - 1],
                    device_id=(grp, blk, planes[by]),
                    device_id_type=MESH,
                )
                for by in (2, 1, 3)
            ])
        return parts

    def block_rows(phase, a):
        return pl.ds(a * TOK, CHUNK - TOK if phase == 0 and a == 1 else TOK)

    def send(source, to, send_sem, recv_sem, device_id):
        return pltpu.make_async_remote_copy(
            src_ref=source,
            dst_ref=to,
            send_sem=send_sem,
            recv_sem=recv_sem,
            device_id=device_id,
            device_id_type=MESH,
        )

    def halo(phase, group, a):
        rows = block_rows(phase, a)
        g, x, y, k = chip(group)
        copies = []
        for by in (1, 2):
            copies.append((
                k >= by,
                send(
                    held.at[phase, group, 0, :, rows],
                    held.at[phase, group, 2 * by, :, rows],
                    halo_send.at[phase, group, a, by - 1],
                    halo_recv.at[phase, group, a, by - 1],
                    device(group, chip_place(g, jnp.maximum(k - by, 0))),
                ),
            ))
        edge = (k <= 1) & (g >= 1)
        near_row = jnp.minimum(y, 1)
        for p in range(1 - a, SIDE):
            copies.append((
                edge,
                send(
                    held.at[phase, group, 0, p, rows],
                    relay.at[phase, group, rows],
                    piece_send.at[phase, group, a, p],
                    relay_recv.at[phase, group],
                    device(group, (g, p, SIDE - 1 - y if a else y)),
                ),
            ))
        if a == 0:
            copies.append((
                edge,
                send(
                    held.at[phase, group, 0, 0, rows],
                    held.at[phase, group, 2 * (near_row + 1), 0, rows],
                    piece_send.at[phase, group, 0, 0],
                    halo_recv.at[phase, group, 0, near_row],
                    device(group, (jnp.maximum(g - 1, 0), *last)),
                ),
            ))
        return copies

    def pass_piece(phase, group, a):
        rows = block_rows(phase, a)
        g, x, y, k = chip(group)
        near_row = jnp.clip(SIDE - 1 - y if a else y, 0, 1)
        condition = (y >= 2) if a else (y <= 1) & (x >= 1)
        return condition & (g >= 1), send(
            relay.at[phase, group, rows],
            held.at[phase, group, 2 * (near_row + 1), x, rows],
            relay_send.at[phase, group],
            halo_recv.at[phase, group, a, near_row],
            device(group, (jnp.maximum(g - 1, 0), *last)),
        )

    def pass_block(phase, group, a):
        rows = block_rows(phase, a)
        g, x, y, k = chip(group)
        return (k == CHIPS - 1) & (g < grps - 1), send(
            held.at[phase, group, 2, :, rows],
            held.at[phase, group, 4, :, rows],
            next_send.at[phase, group, a],
            halo_recv.at[phase, group, a, 1],
            device(group, (g, SIDE - 1, SIDE - 2)),
        )

    def share(phase, group, a):
        rows = block_rows(phase, a)
        side = core if group == 0 else 1 - core
        return [
            send(
                held.at[phase, group, 2 * j + 2 * side, :, rows],
                held.at[phase, group, 2 * j + 1, :, rows],
                sib_send.at[phase, group, a, j],
                sib_recv.at[phase, group, a, j],
                sibling,
            )
            for j in range(2)
        ]

    targets = ((query_grad, out), (key_grad, value_grad))

    def give(phase, group):
        column = pl.ds(pl.multiple_of((2 * me + phase) * DH, DH), DH)
        parts = []
        for n in range(PARTS):
            a, rows = n * PART // TOK, pl.ds(n * PART % TOK, PART)
            parts.append([
                pltpu.make_async_remote_copy(
                    src_ref=result.at[phase, group, a, planes[by], rows],
                    dst_ref=targets[group][a].at[rows, column],
                    send_sem=out_send.at[phase, group, n, by - 1],
                    recv_sem=out_recv.at[phase, group, n, by - 1],
                    device_id=(grp, blk, planes[by]),
                    device_id_type=MESH,
                )
                for by in (2, 1, 3)
            ])
        own = [
            pltpu.make_async_copy(
                result.at[phase, group, a, me],
                targets[group][a].at[:, column],
                own_sem.at[phase, group, a],
            )
            for a in range(2)
        ]
        return parts, own

    score_scale = 1.0 / math.sqrt(DH)
    both_scales = 1.0 / math.sqrt(DH * REACH * BLOCK)
    part = ROWS // TOK

    def unit(phase, group, slot, step, diagonal):
        mine = held.at[phase, 1 - group, 0, pl.ds(step * part, part)]
        theirs = held.at[phase, group, slot]
        first = mine[:, 0:TOK, :].reshape(ROWS, DH)
        second = mine[:, TOK : 2 * TOK, :].reshape(ROWS, DH)
        other_first = theirs[:, 0:TOK, :].reshape(BLOCK, DH)
        other_second = theirs[:, TOK : 2 * TOK, :].reshape(BLOCK, DH)
        their_seg = held[0, group, slot, :, 2 * TOK :, :].astype(jnp.float32)
        at = pl.ds(pl.multiple_of(step * ROWS, ROWS), ROWS)
        my_seg = seg_rows[at, :]
        scores = lax.dot_general(first, other_first, NT, preferred_element_type=jnp.float32)
        dprob = lax.dot_general(second, other_second, NT, preferred_element_type=jnp.float32)
        weights, dscores = [], []
        for p in range(PLANES):
            cols = slice(p * TOK, (p + 1) * TOK)
            allowed = my_seg == their_seg[p, 0:1, :]
            if diagonal:
                row = lax.broadcasted_iota(jnp.int32, (ROWS, TOK), 0) + step * ROWS
                col = lax.broadcasted_iota(jnp.int32, (ROWS, TOK), 1) + p * TOK
                allowed = allowed & ((col <= row) if group == 0 else (row <= col))
            raw = scores[:, cols]
            grown = 1.0 + jnp.exp2(jnp.minimum(raw * (-score_scale * LOG2E), 115.0))
            s = pl.reciprocal(grown, approx=True)
            s = s * (2.0 - grown * s)
            active = raw * s
            slope = s + active * (score_scale - score_scale * s)
            weights.append(jnp.where(allowed, active, 0.0).astype(jnp.bfloat16))
            dscores.append(jnp.where(allowed, dprob[:, cols] * slope, 0.0).astype(jnp.bfloat16))
        weight = jnp.concatenate(weights, axis=1)
        dscore = jnp.concatenate(dscores, axis=1)
        first_term = lax.dot_general(dscore, other_first, NN, preferred_element_type=jnp.float32)
        second_term = lax.dot_general(weight, other_second, NN, preferred_element_type=jnp.float32)
        if diagonal:
            acc[group, 0, at, :] = first_term
            acc[group, 1, at, :] = second_term
        else:
            acc[group, 0, at, :] += first_term
            acc[group, 1, at, :] += second_term

    steps = BLOCK // ROWS

    def diagonal(phase, group):
        def body(step, carry):
            unit(phase, group, 0, step, True)
            return carry

        lax.fori_loop(0, steps, body, 0)

    def others(phase, group):
        def body(i, carry):
            unit(phase, group, 1 + i // steps, lax.rem(i, steps), False)
            return carry

        lax.fori_loop(0, REACH * steps, body, 0)

    def finish(phase, group):
        for a in range(2):
            for p in range(PLANES):
                total = acc[group, a, p * TOK : (p + 1) * TOK, :] * both_scales
                result[phase, group, a, p] = total.astype(jnp.bfloat16)

    exchanges = {pg: exchange(*pg) for pg in groups}
    halves = [(*pg, a) for pg in groups for a in range(2)]
    halos = {half: halo(*half) for half in halves}
    passed = {half: pass_piece(*half) for half in halves}
    seconds = {half: pass_block(*half) for half in halves}
    shares = {half: share(*half) for half in halves}
    gives = {pg: give(*pg) for pg in groups}

    queue = [part for pg in groups for part in exchanges[pg]]
    queue += [part for pg in groups for part in gives[pg][0]]
    window = 3
    issued = []
    gone = []

    def left(count):
        for n in range(len(gone), count):
            for copy in queue[n]:
                copy.wait_send()
            gone.append(n)

    def issue(count, limited=True):
        for n in range(len(issued), len(issued) + count):
            if limited:
                left(n - window + 1)
            if n in (0, 2 * PARTS):
                for group in range(2):
                    for copy in loads[n // (2 * PARTS), group]:
                        copy.wait()
            for copy in queue[n]:
                copy.start()
            issued.append(n)

    def arrive(phase, turn, a):
        for part in exchanges[phase, turn][a * PARTS // 2 : (a + 1) * PARTS // 2]:
            for copy in part:
                copy.wait_recv()

    def start_halo(phase, turn, a):
        for condition, copy in halo(phase, order[phase][turn], a):
            pl.when(condition)(copy.start)

    def hand_on(pg):
        for a in range(2):
            condition, copy = passed[*pg, a]

            @pl.when(condition)
            def _():
                pltpu.make_async_copy(copy.src_ref, copy.src_ref, relay_recv.at[pg]).wait()
                copy.start()

    def forward(pg):
        for a in range(2):
            condition, copy = seconds[*pg, a]

            @pl.when(condition)
            def _():
                halos[*pg, a][0][1].wait_recv()
                copy.start()

    def near(pg):
        for a in range(2):
            inside = comes(pg[1], 1) & ~seconds[*pg, a][0]
            pl.when(inside)(halos[*pg, a][0][1].wait_recv)
            shares[*pg, a][0].start()

    def far(pg):
        for a in range(2):
            pl.when(comes(pg[1], 2))(halos[*pg, a][1][1].wait_recv)
            shares[*pg, a][1].start()
        for a in range(2):
            for copy in shares[*pg, a]:
                copy.wait_recv()

    def start_give(pg):
        finish(*pg)
        for copy in gives[pg][1]:
            copy.start()

    kv_a, qd_a, kv_b, qd_b = groups
    issue(5)
    arrive(0, 0, 0)
    start_halo(0, 0, 0)
    issue(2)
    arrive(0, 0, 1)
    theirs, mine = held.at[0, 0, 0], held.at[0, 1, 0]
    for p in range(PLANES):
        numbers = theirs[p, 2 * TOK :, :]
        mine[p, 2 * TOK :, :] = numbers
        row = numbers.astype(jnp.float32)[0:1, :]
        seg_rows[p * TOK : (p + 1) * TOK, :] = jnp.broadcast_to(row, (TOK, TOK)).T
    start_halo(0, 0, 1)
    issue(1)
    hand_on(kv_a)
    issue(2)
    arrive(0, 1, 0)
    start_halo(0, 1, 0)
    issue(1)
    arrive(0, 1, 1)
    start_halo(0, 1, 1)

    issue(1)
    forward(kv_a)
    near(kv_a)
    diagonal(*kv_a)
    hand_on(qd_a)
    issue(1)
    far(kv_a)
    issue(1)
    arrive(1, 0, 0)
    start_halo(1, 0, 0)
    others(*kv_a)
    start_give(kv_a)
    issue(2)

    arrive(1, 0, 1)
    start_halo(1, 0, 1)
    forward(qd_a)
    near(qd_a)
    diagonal(*qd_a)
    hand_on(kv_b)
    hand_on(qd_b)
    issue(1)
    far(qd_a)
    arrive(1, 1, 0)
    start_halo(1, 1, 0)
    others(*qd_a)
    start_give(qd_a)
    issue(2)

    arrive(1, 1, 1)
    start_halo(1, 1, 1)
    forward(kv_b)
    near(kv_b)
    diagonal(*kv_b)
    forward(qd_b)
    issue(6 * PARTS - len(issued), limited=False)
    far(kv_b)
    others(*kv_b)
    start_give(kv_b)
    issue(PARTS, limited=False)

    near(qd_b)
    diagonal(*qd_b)
    far(qd_b)
    others(*qd_b)
    start_give(qd_b)
    issue(PARTS, limited=False)

    left(len(queue))
    for half in halves:
        for copy in shares[half]:
            copy.wait_send()
        for condition, copy in halos[half] + [passed[half], seconds[half]]:
            pl.when(condition)(copy.wait_send)
    for pg in groups:
        parts, own = gives[pg]
        for part in parts:
            for copy in part:
                copy.wait_recv()
        for copy in own:
            copy.wait()


def hand_over(*refs):
    ins, outs, (here, sems) = refs[:4], refs[4:8], refs[8:]
    arriving = [pltpu.make_async_copy(ins[i], here.at[i], sems.at[0, i]) for i in range(4)]
    leaving = [pltpu.make_async_copy(here.at[i], outs[i], sems.at[1, i]) for i in range(4)]
    for copy in arriving:
        copy.start()
    for i in range(4):
        arriving[i].wait()
        leaving[i].start()
    for copy in leaving:
        copy.wait()


def shards(grps, queries, keys, values, out_grad, segment):
    tokens, features = queries.shape
    shape = jax.ShapeDtypeStruct((tokens, features), jnp.bfloat16)
    anywhere = pl.BlockSpec(memory_space=pl.ANY)
    dma = pltpu.SemaphoreType.DMA
    results = pl.pallas_call(
        functools.partial(kernel, grps),
        out_shape=(shape,) * 4,
        in_specs=[anywhere] * 5,
        out_specs=[anywhere] * 4,
        scratch_shapes=[
            pltpu.VMEM((2, 2, REACH + 1, PLANES, CHUNK, DH), jnp.bfloat16),
            pltpu.VMEM((2, 2, PLANES - 1, CHUNK, DH), jnp.bfloat16),
            pltpu.VMEM((2, 2, 2, PLANES, TOK, DH), jnp.bfloat16),
            pltpu.VMEM((2, 2, BLOCK, DH), jnp.float32),
            pltpu.VMEM((BLOCK, TOK), jnp.float32),
            dma((2, 2, PLANES, 2)),
            dma((2, 2, PARTS, 3)),
            dma((2, 2, PARTS, 3)),
            dma((2, 2, 2, 2)),
            dma((2, 2, 2, 2)),
            dma((2, 2, 2, 2)),
            dma((2, 2, 2, 2)),
            dma((2, 2, PARTS, 3)),
            dma((2, 2, PARTS, 3)),
            dma((2, 2, 2)),
            pltpu.VMEM((2, 2, CHUNK, DH), jnp.bfloat16),
            dma((2, 2, 2, SIDE)),
            dma((2, 2)),
            dma((2, 2)),
            dma((2, 2, 2)),
            dma(()),
            pltpu.VMEM((1, TOK), jnp.int32),
        ],
        compiler_params=pltpu.CompilerParams(
            collective_id=0, has_side_effects=True, vmem_limit_bytes=60 << 20
        ),
        cost_estimate=pl.CostEstimate(
            flops=2 * 2 * 10 * 4 * BLOCK * BLOCK * DH,
            bytes_accessed=8 * tokens * features * 2,
            transcendentals=2 * 10 * BLOCK * BLOCK,
        ),
    )(queries, keys, values, out_grad, segment.reshape(1, tokens))
    return pl.pallas_call(
        hand_over,
        out_shape=(shape,) * 4,
        in_specs=[anywhere] * 4,
        out_specs=[anywhere] * 4,
        scratch_shapes=[pltpu.VMEM((4, tokens, features), jnp.bfloat16), dma((2, 4))],
        compiler_params=pltpu.CompilerParams(vmem_limit_bytes=60 << 20),
    )(*results)


def solution(mesh):
    rows = P(("grp", "blk", "head"), None)
    return jax.shard_map(
        functools.partial(shards, mesh.shape["grp"]),
        mesh=mesh,
        in_specs=(rows, rows, rows, rows, P(("grp", "blk", "head"))),
        out_specs=(rows,) * 4,
        check_vma=False,
    )
```

```python
import functools
import math

import jax
import jax.numpy as jnp
from jax import lax
from jax.experimental import pallas as pl
from jax.experimental.pallas import tpu as pltpu
from jax.sharding import PartitionSpec as P

MESH = pl.DeviceIdType.MESH
LOG2E = math.log2(math.e)
DH = 128
REACH = 4
TOK = 128
PLANES = 4
BLOCK = TOK * PLANES
CHUNK = 2 * TOK + 16
PART = 64
PARTS = 2 * TOK // PART
ROWS = 512
NT = (((1,), (1,)), ((), ()))
NN = (((1,), (0,)), ((), ()))


SIDE = 4
CHIPS = SIDE * SIDE


def kernel(
    grps,
    queries, keys, values, out_grad, segment,
    out, query_grad, key_grad, value_grad,
    held, stage, result, acc, seg_rows,
    load_sem, in_send, in_recv, halo_send, halo_recv, sib_send, sib_recv, out_send, out_recv, own_sem,
    relay, piece_send, relay_recv, relay_send, next_send, seg_sem, seg_here,
):
    grp, blk, me = lax.axis_index("grp"), lax.axis_index("blk"), lax.axis_index("head")
    core = lax.rem(blk, 2)
    sibling = (grp, blk + 1 - 2 * core, me)
    planes = [lax.rem(me + by, PLANES) for by in range(PLANES)]

    def mirrored(group, place):
        turned = [n - 1 - at for n, at in zip((grps, SIDE, SIDE), place)]
        if isinstance(group, int):
            return tuple(place if group else turned)
        return tuple(jnp.where(group == 1, *pair) for pair in zip(place, turned))

    def device(group, place):
        g, x, y = mirrored(group, place)
        return (g, (x * SIDE + y) * 2 + core, me)

    here = (grp, blk // (2 * SIDE), lax.rem(blk // 2, SIDE))

    def chip(group):
        g, x, y = mirrored(group, here)
        return g, x, y, x * SIDE + y

    def chip_place(g, k):
        return g, k // SIDE, lax.rem(k, SIDE)

    last = (SIDE - 1, SIDE - 1)

    first = jnp.where((chip(1)[3] <= 1) & (grp >= 1), 1, 0)
    order = ((0, 1), (first, 1 - first))

    sources = ((keys, values), (queries, out_grad))
    groups = ((0, 0), (0, 1), (1, 0), (1, 1))

    def load(phase, group):
        copies = []
        for by in range(PLANES):
            plane = planes[by]
            column = pl.ds(pl.multiple_of((2 * plane + phase) * DH, DH), DH)
            for a in range(2):
                if by == 0:
                    to = held.at[phase, group, 0, me, pl.ds(a * TOK, TOK)]
                else:
                    to = stage.at[phase, group, by - 1, pl.ds(a * TOK, TOK)]
                copies.append(
                    pltpu.make_async_copy(
                        sources[group][a].at[:, column], to, load_sem.at[phase, group, by, a]
                    )
                )
        return copies

    loads = {pg: load(*pg) for pg in groups}
    for pg in groups:
        for copy in loads[pg]:
            copy.start()

    seg_load = pltpu.make_async_copy(segment, seg_here, seg_sem)
    seg_load.start()

    barrier = pltpu.get_barrier_semaphore()

    def greet(to):
        pl.semaphore_signal(barrier, inc=1, device_id=to, device_id_type=MESH)

    for by in range(1, PLANES):
        greet((grp, blk, planes[by]))
    greet(sibling)
    greeted = PLANES

    def greet_if(condition, partners):
        @pl.when(condition)
        def _():
            for partner in partners:
                greet(partner)

        return jnp.where(condition, len(partners), 0)

    for group in range(2):
        g, x, y, k = chip(group)
        for by in (1, 2):
            greeted += greet_if(k >= by, [device(group, chip_place(g, k - by))])
            greeted += greet_if(k < CHIPS - by, [device(group, chip_place(g, k + by))])
        greeted += greet_if(
            (x == 0) & (y <= 1) & (g >= 1),
            [device(group, (g, p, y)) for p in range(1, SIDE)]
            + [device(group, (g, p, SIDE - 1 - y)) for p in range(SIDE)],
        )
        greeted += greet_if((x > 0) & (y <= 1) & (g >= 1), [device(group, (g, 0, y))])
        greeted += greet_if((y >= 2) & (g >= 1), [device(group, (g, 0, SIDE - 1 - y))])
        greeted += greet_if(g >= 1, [device(group, (g - 1, *last))])
        greeted += greet_if(
            (k == CHIPS - 1) & (g < grps - 1),
            [device(group, (g + 1, p, row)) for p in range(SIDE) for row in range(SIDE)],
        )

    def blank(group, slot):
        for phase in range(2):
            held[phase, group, slot, :, 0 : 2 * TOK, :] = jnp.zeros(
                (PLANES, 2 * TOK, DH), jnp.bfloat16
            )
        held[0, group, slot, :, 2 * TOK :, :] = jnp.full((PLANES, 16, DH), -1, jnp.bfloat16)

    def comes(group, by):
        g, x, y, k = chip(group)
        return (g < grps - 1) | (k < CHIPS - by)

    for group in range(2):
        for by in (1, 2):
            pl.when(~comes(group, by))(functools.partial(blank, group, 2 * by))

    seg_load.wait()
    seg = jnp.broadcast_to(seg_here[...].astype(jnp.float32), (16, TOK)).astype(jnp.bfloat16)
    for by in range(3):
        stage[0, 0, by, 2 * TOK :, :] = seg
    held[0, 0, 0, me, 2 * TOK :, :] = seg

    pl.semaphore_wait(barrier, greeted)

    def exchange(phase, turn):
        group = order[phase][turn]
        total = CHUNK if phase == turn == 0 else 2 * TOK
        parts = []
        for n in range(PARTS):
            rows = pl.ds(n * PART, total - n * PART if n == PARTS - 1 else PART)
            parts.append([
                pltpu.make_async_remote_copy(
                    src_ref=stage.at[phase, group, by - 1, rows],
                    dst_ref=held.at[phase, group, 0, me, rows],
                    send_sem=in_send.at[phase, group, n, by - 1],
                    recv_sem=in_recv.at[phase, group, n, by - 1],
                    device_id=(grp, blk, planes[by]),
                    device_id_type=MESH,
                )
                for by in (2, 1, 3)
            ])
        return parts

    def block_rows(phase, a):
        return pl.ds(a * TOK, CHUNK - TOK if phase == 0 and a == 1 else TOK)

    def send(source, to, send_sem, recv_sem, device_id):
        return pltpu.make_async_remote_copy(
            src_ref=source,
            dst_ref=to,
            send_sem=send_sem,
            recv_sem=recv_sem,
            device_id=device_id,
            device_id_type=MESH,
        )

    def halo(phase, group, a):
        rows = block_rows(phase, a)
        g, x, y, k = chip(group)
        copies = []
        for by in (1, 2):
            copies.append((
                k >= by,
                send(
                    held.at[phase, group, 0, :, rows],
                    held.at[phase, group, 2 * by, :, rows],
                    halo_send.at[phase, group, a, by - 1],
                    halo_recv.at[phase, group, a, by - 1],
                    device(group, chip_place(g, jnp.maximum(k - by, 0))),
                ),
            ))
        edge = (k <= 1) & (g >= 1)
        near_row = jnp.minimum(y, 1)
        for p in range(1 - a, SIDE):
            copies.append((
                edge,
                send(
                    held.at[phase, group, 0, p, rows],
                    relay.at[phase, group, rows],
                    piece_send.at[phase, group, a, p],
                    relay_recv.at[phase, group],
                    device(group, (g, p, SIDE - 1 - y if a else y)),
                ),
            ))
        if a == 0:
            copies.append((
                edge,
                send(
                    held.at[phase, group, 0, 0, rows],
                    held.at[phase, group, 2 * (near_row + 1), 0, rows],
                    piece_send.at[phase, group, 0, 0],
                    halo_recv.at[phase, group, 0, near_row],
                    device(group, (jnp.maximum(g - 1, 0), *last)),
                ),
            ))
        return copies

    def pass_piece(phase, group, a):
        rows = block_rows(phase, a)
        g, x, y, k = chip(group)
        near_row = jnp.clip(SIDE - 1 - y if a else y, 0, 1)
        condition = (y >= 2) if a else (y <= 1) & (x >= 1)
        return condition & (g >= 1), send(
            relay.at[phase, group, rows],
            held.at[phase, group, 2 * (near_row + 1), x, rows],
            relay_send.at[phase, group],
            halo_recv.at[phase, group, a, near_row],
            device(group, (jnp.maximum(g - 1, 0), *last)),
        )

    def pass_block(phase, group, a):
        rows = block_rows(phase, a)
        g, x, y, k = chip(group)
        return (k == CHIPS - 1) & (g < grps - 1), send(
            held.at[phase, group, 2, :, rows],
            held.at[phase, group, 4, :, rows],
            next_send.at[phase, group, a],
            halo_recv.at[phase, group, a, 1],
            device(group, (g, SIDE - 1, SIDE - 2)),
        )

    def share(phase, group, a):
        rows = block_rows(phase, a)
        side = core if group == 0 else 1 - core
        return [
            send(
                held.at[phase, group, 2 * j + 2 * side, :, rows],
                held.at[phase, group, 2 * j + 1, :, rows],
                sib_send.at[phase, group, a, j],
                sib_recv.at[phase, group, a, j],
                sibling,
            )
            for j in range(2)
        ]

    targets = ((query_grad, out), (key_grad, value_grad))

    def give(phase, group):
        column = pl.ds(pl.multiple_of((2 * me + phase) * DH, DH), DH)
        parts = []
        for n in range(PARTS):
            a, rows = n * PART // TOK, pl.ds(n * PART % TOK, PART)
            parts.append([
                pltpu.make_async_remote_copy(
                    src_ref=result.at[phase, group, a, planes[by], rows],
                    dst_ref=targets[group][a].at[rows, column],
                    send_sem=out_send.at[phase, group, n, by - 1],
                    recv_sem=out_recv.at[phase, group, n, by - 1],
                    device_id=(grp, blk, planes[by]),
                    device_id_type=MESH,
                )
                for by in (2, 1, 3)
            ])
        own = [
            pltpu.make_async_copy(
                result.at[phase, group, a, me],
                targets[group][a].at[:, column],
                own_sem.at[phase, group, a],
            )
            for a in range(2)
        ]
        return parts, own

    score_scale = 1.0 / math.sqrt(DH)
    both_scales = 1.0 / math.sqrt(DH * REACH * BLOCK)
    part = ROWS // TOK

    def unit(phase, group, slot, step, diagonal):
        mine = held.at[phase, 1 - group, 0, pl.ds(step * part, part)]
        theirs = held.at[phase, group, slot]
        first = mine[:, 0:TOK, :].reshape(ROWS, DH)
        second = mine[:, TOK : 2 * TOK, :].reshape(ROWS, DH)
        other_first = theirs[:, 0:TOK, :].reshape(BLOCK, DH)
        other_second = theirs[:, TOK : 2 * TOK, :].reshape(BLOCK, DH)
        their_seg = held[0, group, slot, :, 2 * TOK :, :].astype(jnp.float32)
        at = pl.ds(pl.multiple_of(step * ROWS, ROWS), ROWS)
        my_seg = seg_rows[at, :]
        scores = lax.dot_general(first, other_first, NT, preferred_element_type=jnp.float32)
        dprob = lax.dot_general(second, other_second, NT, preferred_element_type=jnp.float32)
        weights, dscores = [], []
        for p in range(PLANES):
            cols = slice(p * TOK, (p + 1) * TOK)
            allowed = my_seg == their_seg[p, 0:1, :]
            if diagonal:
                row = lax.broadcasted_iota(jnp.int32, (ROWS, TOK), 0) + step * ROWS
                col = lax.broadcasted_iota(jnp.int32, (ROWS, TOK), 1) + p * TOK
                allowed = allowed & ((col <= row) if group == 0 else (row <= col))
            raw = scores[:, cols]
            grown = 1.0 + jnp.exp2(jnp.minimum(raw * (-score_scale * LOG2E), 115.0))
            s = pl.reciprocal(grown, approx=True)
            s = s * (2.0 - grown * s)
            active = raw * s
            slope = s + active * (score_scale - score_scale * s)
            weights.append(jnp.where(allowed, active, 0.0).astype(jnp.bfloat16))
            dscores.append(jnp.where(allowed, dprob[:, cols] * slope, 0.0).astype(jnp.bfloat16))
        weight = jnp.concatenate(weights, axis=1)
        dscore = jnp.concatenate(dscores, axis=1)
        first_term = lax.dot_general(dscore, other_first, NN, preferred_element_type=jnp.float32)
        second_term = lax.dot_general(weight, other_second, NN, preferred_element_type=jnp.float32)
        if diagonal:
            acc[group, 0, at, :] = first_term
            acc[group, 1, at, :] = second_term
        else:
            acc[group, 0, at, :] += first_term
            acc[group, 1, at, :] += second_term

    steps = BLOCK // ROWS

    def diagonal(phase, group):
        def body(step, carry):
            unit(phase, group, 0, step, True)
            return carry

        lax.fori_loop(0, steps, body, 0)

    def others(phase, group, upper):
        def body(i, carry):
            unit(phase, group, upper - i // steps, lax.rem(i, steps), False)
            return carry

        lax.fori_loop(0, 2 * steps, body, 0)

    def finish(phase, group):
        for a in range(2):
            for p in range(PLANES):
                total = acc[group, a, p * TOK : (p + 1) * TOK, :] * both_scales
                result[phase, group, a, p] = total.astype(jnp.bfloat16)

    exchanges = {pg: exchange(*pg) for pg in groups}
    halves = [(*pg, a) for pg in groups for a in range(2)]
    halos = {half: halo(*half) for half in halves}
    passed = {half: pass_piece(*half) for half in halves}
    seconds = {half: pass_block(*half) for half in halves}
    shares = {half: share(*half) for half in halves}
    gives = {pg: give(*pg) for pg in groups}

    queue = [part for pg in groups for part in exchanges[pg]]
    queue += [part for pg in groups for part in gives[pg][0]]
    window = 3
    issued = []
    gone = []

    def left(count):
        for n in range(len(gone), count):
            for copy in queue[n]:
                copy.wait_send()
            gone.append(n)

    def issue(count, limited=True):
        for n in range(len(issued), len(issued) + count):
            if limited:
                left(n - window + 1)
            if n in (0, 2 * PARTS):
                for group in range(2):
                    for copy in loads[n // (2 * PARTS), group]:
                        copy.wait()
            for copy in queue[n]:
                copy.start()
            issued.append(n)

    def arrive(phase, turn, a):
        for part in exchanges[phase, turn][a * PARTS // 2 : (a + 1) * PARTS // 2]:
            for copy in part:
                copy.wait_recv()

    def start_halo(phase, turn, a):
        for condition, copy in halo(phase, order[phase][turn], a):
            pl.when(condition)(copy.start)

    def hand_on(pg):
        for a in range(2):
            condition, copy = passed[*pg, a]

            @pl.when(condition)
            def _():
                pltpu.make_async_copy(copy.src_ref, copy.src_ref, relay_recv.at[pg]).wait()
                copy.start()

    def forward(pg):
        for a in range(2):
            condition, copy = seconds[*pg, a]

            @pl.when(condition)
            def _():
                halos[*pg, a][0][1].wait_recv()
                copy.start()

    def near(pg):
        for a in range(2):
            inside = comes(pg[1], 1) & ~seconds[*pg, a][0]
            pl.when(inside)(halos[*pg, a][0][1].wait_recv)
            shares[*pg, a][0].start()

    def middle(pg):
        diagonal(*pg)
        for a in range(2):
            shares[*pg, a][0].wait_recv()
        others(*pg, 2)

    def far(pg):
        for a in range(2):
            pl.when(comes(pg[1], 2))(halos[*pg, a][1][1].wait_recv)
            shares[*pg, a][1].start()
        for a in range(2):
            shares[*pg, a][1].wait_recv()
        others(*pg, 4)

    def start_give(pg):
        finish(*pg)
        for copy in gives[pg][1]:
            copy.start()

    kv_a, qd_a, kv_b, qd_b = groups
    issue(5)
    arrive(0, 0, 0)
    start_halo(0, 0, 0)
    issue(2)
    arrive(0, 0, 1)
    theirs, mine = held.at[0, 0, 0], held.at[0, 1, 0]
    for p in range(PLANES):
        numbers = theirs[p, 2 * TOK :, :]
        mine[p, 2 * TOK :, :] = numbers
        row = numbers.astype(jnp.float32)[0:1, :]
        seg_rows[p * TOK : (p + 1) * TOK, :] = jnp.broadcast_to(row, (TOK, TOK)).T
    start_halo(0, 0, 1)
    issue(1)
    hand_on(kv_a)
    issue(2)
    arrive(0, 1, 0)
    start_halo(0, 1, 0)
    issue(1)
    arrive(0, 1, 1)
    start_halo(0, 1, 1)

    issue(1)
    forward(kv_a)
    near(kv_a)
    hand_on(qd_a)
    middle(kv_a)
    issue(2)
    arrive(1, 0, 0)
    start_halo(1, 0, 0)
    far(kv_a)
    start_give(kv_a)
    issue(2)

    arrive(1, 0, 1)
    start_halo(1, 0, 1)
    forward(qd_a)
    near(qd_a)
    middle(qd_a)
    hand_on(kv_b)
    hand_on(qd_b)
    issue(1)
    arrive(1, 1, 0)
    start_halo(1, 1, 0)
    far(qd_a)
    start_give(qd_a)
    issue(2)

    arrive(1, 1, 1)
    start_halo(1, 1, 1)
    forward(kv_b)
    near(kv_b)
    middle(kv_b)
    forward(qd_b)
    issue(6 * PARTS - len(issued), limited=False)
    far(kv_b)
    start_give(kv_b)
    issue(PARTS, limited=False)

    near(qd_b)
    middle(qd_b)
    far(qd_b)
    start_give(qd_b)
    issue(PARTS, limited=False)

    left(len(queue))
    for half in halves:
        for copy in shares[half]:
            copy.wait_send()
        for condition, copy in halos[half] + [passed[half], seconds[half]]:
            pl.when(condition)(copy.wait_send)
    for pg in groups:
        parts, own = gives[pg]
        for part in parts:
            for copy in part:
                copy.wait_recv()
        for copy in own:
            copy.wait()


def hand_over(*refs):
    ins, outs, (here, sems) = refs[:4], refs[4:8], refs[8:]
    arriving = [pltpu.make_async_copy(ins[i], here.at[i], sems.at[0, i]) for i in range(4)]
    leaving = [pltpu.make_async_copy(here.at[i], outs[i], sems.at[1, i]) for i in range(4)]
    for copy in arriving:
        copy.start()
    for i in range(4):
        arriving[i].wait()
        leaving[i].start()
    for copy in leaving:
        copy.wait()


def shards(grps, queries, keys, values, out_grad, segment):
    tokens, features = queries.shape
    shape = jax.ShapeDtypeStruct((tokens, features), jnp.bfloat16)
    anywhere = pl.BlockSpec(memory_space=pl.ANY)
    dma = pltpu.SemaphoreType.DMA
    results = pl.pallas_call(
        functools.partial(kernel, grps),
        out_shape=(shape,) * 4,
        in_specs=[anywhere] * 5,
        out_specs=[anywhere] * 4,
        scratch_shapes=[
            pltpu.VMEM((2, 2, REACH + 1, PLANES, CHUNK, DH), jnp.bfloat16),
            pltpu.VMEM((2, 2, PLANES - 1, CHUNK, DH), jnp.bfloat16),
            pltpu.VMEM((2, 2, 2, PLANES, TOK, DH), jnp.bfloat16),
            pltpu.VMEM((2, 2, BLOCK, DH), jnp.float32),
            pltpu.VMEM((BLOCK, TOK), jnp.float32),
            dma((2, 2, PLANES, 2)),
            dma((2, 2, PARTS, 3)),
            dma((2, 2, PARTS, 3)),
            dma((2, 2, 2, 2)),
            dma((2, 2, 2, 2)),
            dma((2, 2, 2, 2)),
            dma((2, 2, 2, 2)),
            dma((2, 2, PARTS, 3)),
            dma((2, 2, PARTS, 3)),
            dma((2, 2, 2)),
            pltpu.VMEM((2, 2, CHUNK, DH), jnp.bfloat16),
            dma((2, 2, 2, SIDE)),
            dma((2, 2)),
            dma((2, 2)),
            dma((2, 2, 2)),
            dma(()),
            pltpu.VMEM((1, TOK), jnp.int32),
        ],
        compiler_params=pltpu.CompilerParams(
            collective_id=0, has_side_effects=True, vmem_limit_bytes=60 << 20
        ),
        cost_estimate=pl.CostEstimate(
            flops=2 * 2 * 10 * 4 * BLOCK * BLOCK * DH,
            bytes_accessed=8 * tokens * features * 2,
            transcendentals=2 * 10 * BLOCK * BLOCK,
        ),
    )(queries, keys, values, out_grad, segment.reshape(1, tokens))
    return pl.pallas_call(
        hand_over,
        out_shape=(shape,) * 4,
        in_specs=[anywhere] * 4,
        out_specs=[anywhere] * 4,
        scratch_shapes=[pltpu.VMEM((4, tokens, features), jnp.bfloat16), dma((2, 4))],
        compiler_params=pltpu.CompilerParams(vmem_limit_bytes=60 << 20),
    )(*results)


def solution(mesh):
    rows = P(("grp", "blk", "head"), None)
    return jax.shard_map(
        functools.partial(shards, mesh.shape["grp"]),
        mesh=mesh,
        in_specs=(rows, rows, rows, rows, P(("grp", "blk", "head"))),
        out_specs=(rows,) * 4,
        check_vma=False,
    )
```

```python
import functools
import math

import jax
import jax.numpy as jnp
from jax import lax
from jax.experimental import pallas as pl
from jax.experimental.pallas import tpu as pltpu
from jax.sharding import PartitionSpec as P

MESH = pl.DeviceIdType.MESH
LOG2E = math.log2(math.e)
DH = 128
REACH = 4
TOK = 128
PLANES = 4
BLOCK = TOK * PLANES
CHUNK = 2 * TOK + 16
PART = 64
PARTS = 2 * TOK // PART
ROWS = 512
NT = (((1,), (1,)), ((), ()))
NN = (((1,), (0,)), ((), ()))


SIDE = 4
CHIPS = SIDE * SIDE


def kernel(
    grps,
    queries, keys, values, out_grad, segment,
    out, query_grad, key_grad, value_grad,
    held, stage, result, acc, seg_rows,
    load_sem, in_send, in_recv, halo_send, halo_recv, sib_send, sib_recv, out_send, out_recv, own_sem,
    relay, piece_send, relay_recv, relay_send, next_send, seg_sem, seg_here,
):
    grp, blk, me = lax.axis_index("grp"), lax.axis_index("blk"), lax.axis_index("head")
    core = lax.rem(blk, 2)
    sibling = (grp, blk + 1 - 2 * core, me)
    planes = [lax.rem(me + by, PLANES) for by in range(PLANES)]

    def mirrored(group, place):
        turned = [n - 1 - at for n, at in zip((grps, SIDE, SIDE), place)]
        if isinstance(group, int):
            return tuple(place if group else turned)
        return tuple(jnp.where(group == 1, *pair) for pair in zip(place, turned))

    def device(group, place):
        g, x, y = mirrored(group, place)
        return (g, (x * SIDE + y) * 2 + core, me)

    here = (grp, blk // (2 * SIDE), lax.rem(blk // 2, SIDE))

    def chip(group):
        g, x, y = mirrored(group, here)
        return g, x, y, x * SIDE + y

    def chip_place(g, k):
        return g, k // SIDE, lax.rem(k, SIDE)

    last = (SIDE - 1, SIDE - 1)

    first = jnp.where((chip(1)[3] <= 1) & (grp >= 1), 1, 0)
    order = ((0, 1), (first, 1 - first))

    sources = ((keys, values), (queries, out_grad))
    groups = ((0, 0), (0, 1), (1, 0), (1, 1))

    def load(phase, group):
        copies = []
        for by in range(PLANES):
            plane = planes[by]
            column = pl.ds(pl.multiple_of((2 * plane + phase) * DH, DH), DH)
            for a in range(2):
                if by == 0:
                    to = held.at[phase, group, 0, me, pl.ds(a * TOK, TOK)]
                else:
                    to = stage.at[phase, group, by - 1, pl.ds(a * TOK, TOK)]
                copies.append(
                    pltpu.make_async_copy(
                        sources[group][a].at[:, column], to, load_sem.at[phase, group, by, a]
                    )
                )
        return copies

    loads = {pg: load(*pg) for pg in groups}
    for pg in groups:
        for copy in loads[pg]:
            copy.start()

    seg_load = pltpu.make_async_copy(segment, seg_here, seg_sem)
    seg_load.start()

    barrier = pltpu.get_barrier_semaphore()

    def greet(to):
        pl.semaphore_signal(barrier, inc=1, device_id=to, device_id_type=MESH)

    for by in range(1, PLANES):
        greet((grp, blk, planes[by]))
    greet(sibling)
    greeted = PLANES

    def greet_if(condition, partners):
        @pl.when(condition)
        def _():
            for partner in partners:
                greet(partner)

        return jnp.where(condition, len(partners), 0)

    for group in range(2):
        g, x, y, k = chip(group)
        for by in (1, 2):
            greeted += greet_if(k >= by, [device(group, chip_place(g, k - by))])
            greeted += greet_if(k < CHIPS - by, [device(group, chip_place(g, k + by))])
        greeted += greet_if(
            (x == 0) & (y <= 1) & (g >= 1),
            [device(group, (g, p, y)) for p in range(1, SIDE)]
            + [device(group, (g, p, SIDE - 1 - y)) for p in range(SIDE)],
        )
        greeted += greet_if((x > 0) & (y <= 1) & (g >= 1), [device(group, (g, 0, y))])
        greeted += greet_if((y >= 2) & (g >= 1), [device(group, (g, 0, SIDE - 1 - y))])
        greeted += greet_if(g >= 1, [device(group, (g - 1, *last))])
        greeted += greet_if(
            (k == CHIPS - 1) & (g < grps - 1),
            [device(group, (g + 1, p, row)) for p in range(SIDE) for row in range(SIDE)],
        )

    def blank(group, slot):
        for phase in range(2):
            held[phase, group, slot, :, 0 : 2 * TOK, :] = jnp.zeros(
                (PLANES, 2 * TOK, DH), jnp.bfloat16
            )
        held[0, group, slot, :, 2 * TOK :, :] = jnp.full((PLANES, 16, DH), -1, jnp.bfloat16)

    def comes(group, by):
        g, x, y, k = chip(group)
        return (g < grps - 1) | (k < CHIPS - by)

    for group in range(2):
        for by in (1, 2):
            pl.when(~comes(group, by))(functools.partial(blank, group, 2 * by))

    seg_load.wait()
    seg = jnp.broadcast_to(seg_here[...].astype(jnp.float32), (16, TOK)).astype(jnp.bfloat16)
    for by in range(3):
        stage[0, 0, by, 2 * TOK :, :] = seg
    held[0, 0, 0, me, 2 * TOK :, :] = seg

    pl.semaphore_wait(barrier, greeted)

    def exchange(phase, turn):
        group = order[phase][turn]
        total = CHUNK if phase == turn == 0 else 2 * TOK
        parts = []
        for n in range(PARTS):
            rows = pl.ds(n * PART, total - n * PART if n == PARTS - 1 else PART)
            parts.append([
                pltpu.make_async_remote_copy(
                    src_ref=stage.at[phase, group, by - 1, rows],
                    dst_ref=held.at[phase, group, 0, me, rows],
                    send_sem=in_send.at[phase, group, n, by - 1],
                    recv_sem=in_recv.at[phase, group, n, by - 1],
                    device_id=(grp, blk, planes[by]),
                    device_id_type=MESH,
                )
                for by in (2, 1, 3)
            ])
        return parts

    def block_rows(phase, a):
        return pl.ds(a * TOK, CHUNK - TOK if phase == 0 and a == 1 else TOK)

    def send(source, to, send_sem, recv_sem, device_id):
        return pltpu.make_async_remote_copy(
            src_ref=source,
            dst_ref=to,
            send_sem=send_sem,
            recv_sem=recv_sem,
            device_id=device_id,
            device_id_type=MESH,
        )

    def halo(phase, group, a):
        rows = block_rows(phase, a)
        g, x, y, k = chip(group)
        copies = []
        for by in (1, 2):
            copies.append((
                k >= by,
                send(
                    held.at[phase, group, 0, :, rows],
                    held.at[phase, group, 2 * by, :, rows],
                    halo_send.at[phase, group, a, by - 1],
                    halo_recv.at[phase, group, a, by - 1],
                    device(group, chip_place(g, jnp.maximum(k - by, 0))),
                ),
            ))
        edge = (k <= 1) & (g >= 1)
        near_row = jnp.minimum(y, 1)
        for p in range(1 - a, SIDE):
            copies.append((
                edge,
                send(
                    held.at[phase, group, 0, p, rows],
                    relay.at[phase, group, rows],
                    piece_send.at[phase, group, a, p],
                    relay_recv.at[phase, group],
                    device(group, (g, p, SIDE - 1 - y if a else y)),
                ),
            ))
        if a == 0:
            copies.append((
                edge,
                send(
                    held.at[phase, group, 0, 0, rows],
                    held.at[phase, group, 2 * (near_row + 1), 0, rows],
                    piece_send.at[phase, group, 0, 0],
                    halo_recv.at[phase, group, 0, near_row],
                    device(group, (jnp.maximum(g - 1, 0), *last)),
                ),
            ))
        return copies

    def pass_piece(phase, group, a):
        rows = block_rows(phase, a)
        g, x, y, k = chip(group)
        near_row = jnp.clip(SIDE - 1 - y if a else y, 0, 1)
        condition = (y >= 2) if a else (y <= 1) & (x >= 1)
        return condition & (g >= 1), send(
            relay.at[phase, group, rows],
            held.at[phase, group, 2 * (near_row + 1), x, rows],
            relay_send.at[phase, group],
            halo_recv.at[phase, group, a, near_row],
            device(group, (jnp.maximum(g - 1, 0), *last)),
        )

    def pass_block(phase, group, a):
        rows = block_rows(phase, a)
        g, x, y, k = chip(group)
        return (k == CHIPS - 1) & (g < grps - 1), send(
            held.at[phase, group, 2, :, rows],
            held.at[phase, group, 4, :, rows],
            next_send.at[phase, group, a],
            halo_recv.at[phase, group, a, 1],
            device(group, (g, SIDE - 1, SIDE - 2)),
        )

    def share(phase, group, a):
        rows = block_rows(phase, a)
        side = core if group == 0 else 1 - core
        return [
            send(
                held.at[phase, group, 2 * j + 2 * side, :, rows],
                held.at[phase, group, 2 * j + 1, :, rows],
                sib_send.at[phase, group, a, j],
                sib_recv.at[phase, group, a, j],
                sibling,
            )
            for j in range(2)
        ]

    targets = ((query_grad, out), (key_grad, value_grad))

    def give(phase, group):
        column = pl.ds(pl.multiple_of((2 * me + phase) * DH, DH), DH)
        parts = []
        for n in range(PARTS):
            a, rows = n * PART // TOK, pl.ds(n * PART % TOK, PART)
            parts.append([
                pltpu.make_async_remote_copy(
                    src_ref=result.at[phase, group, a, planes[by], rows],
                    dst_ref=targets[group][a].at[rows, column],
                    send_sem=out_send.at[phase, group, n, by - 1],
                    recv_sem=out_recv.at[phase, group, n, by - 1],
                    device_id=(grp, blk, planes[by]),
                    device_id_type=MESH,
                )
                for by in (2, 1, 3)
            ])
        own = [
            pltpu.make_async_copy(
                result.at[phase, group, a, me],
                targets[group][a].at[:, column],
                own_sem.at[phase, group, a],
            )
            for a in range(2)
        ]
        return parts, own

    score_scale = 1.0 / math.sqrt(DH)
    both_scales = 1.0 / math.sqrt(DH * REACH * BLOCK)
    part = ROWS // TOK

    def unit(phase, group, slot, step, diagonal):
        mine = held.at[phase, 1 - group, 0, pl.ds(step * part, part)]
        theirs = held.at[phase, group, slot]
        first = mine[:, 0:TOK, :].reshape(ROWS, DH)
        second = mine[:, TOK : 2 * TOK, :].reshape(ROWS, DH)
        other_first = theirs[:, 0:TOK, :].reshape(BLOCK, DH)
        other_second = theirs[:, TOK : 2 * TOK, :].reshape(BLOCK, DH)
        their_seg = held[0, group, slot, :, 2 * TOK :, :].astype(jnp.float32)
        at = pl.ds(pl.multiple_of(step * ROWS, ROWS), ROWS)
        my_seg = seg_rows[at, :]
        scores = lax.dot_general(first, other_first, NT, preferred_element_type=jnp.float32)
        dprob = lax.dot_general(second, other_second, NT, preferred_element_type=jnp.float32)
        weights, dscores = [], []
        for p in range(PLANES):
            cols = slice(p * TOK, (p + 1) * TOK)
            allowed = my_seg == their_seg[p, 0:1, :]
            if diagonal:
                row = lax.broadcasted_iota(jnp.int32, (ROWS, TOK), 0) + step * ROWS
                col = lax.broadcasted_iota(jnp.int32, (ROWS, TOK), 1) + p * TOK
                allowed = allowed & ((col <= row) if group == 0 else (row <= col))
            raw = scores[:, cols]
            grown = 1.0 + jnp.exp2(jnp.minimum(raw * (-score_scale * LOG2E), 115.0))
            s = pl.reciprocal(grown, approx=True)
            s = s * (2.0 - grown * s)
            active = raw * s
            slope = s + active * (score_scale - score_scale * s)
            weights.append(jnp.where(allowed, active, 0.0).astype(jnp.bfloat16))
            dscores.append(jnp.where(allowed, dprob[:, cols] * slope, 0.0).astype(jnp.bfloat16))
        weight = jnp.concatenate(weights, axis=1)
        dscore = jnp.concatenate(dscores, axis=1)
        first_term = lax.dot_general(dscore, other_first, NN, preferred_element_type=jnp.float32)
        second_term = lax.dot_general(weight, other_second, NN, preferred_element_type=jnp.float32)
        if diagonal:
            acc[group, 0, at, :] = first_term
            acc[group, 1, at, :] = second_term
        else:
            acc[group, 0, at, :] += first_term
            acc[group, 1, at, :] += second_term

    steps = BLOCK // ROWS

    def diagonal(phase, group):
        def body(step, carry):
            unit(phase, group, 0, step, True)
            return carry

        lax.fori_loop(0, steps, body, 0)

    def others(phase, group, upper):
        def body(i, carry):
            unit(phase, group, upper - i // steps, lax.rem(i, steps), False)
            return carry

        lax.fori_loop(0, 2 * steps, body, 0)

    def finish(phase, group):
        for a in range(2):
            for p in range(PLANES):
                total = acc[group, a, p * TOK : (p + 1) * TOK, :] * both_scales
                result[phase, group, a, p] = total.astype(jnp.bfloat16)

    exchanges = {pg: exchange(*pg) for pg in groups}
    halves = [(*pg, a) for pg in groups for a in range(2)]
    halos = {half: halo(*half) for half in halves}
    passed = {half: pass_piece(*half) for half in halves}
    seconds = {half: pass_block(*half) for half in halves}
    shares = {half: share(*half) for half in halves}
    gives = {pg: give(*pg) for pg in groups}

    queue = [part for pg in groups for part in exchanges[pg]]
    queue += [part for pg in groups for part in gives[pg][0]]
    window = 3
    issued = []
    gone = []

    def left(count):
        for n in range(len(gone), count):
            for copy in queue[n]:
                copy.wait_send()
            gone.append(n)

    def issue(count, limited=True):
        for n in range(len(issued), len(issued) + count):
            if limited:
                left(n - window + 1)
            if n in (0, 2 * PARTS):
                for group in range(2):
                    for copy in loads[n // (2 * PARTS), group]:
                        copy.wait()
            for copy in queue[n]:
                copy.start()
            issued.append(n)

    def arrive(phase, turn, a):
        for part in exchanges[phase, turn][a * PARTS // 2 : (a + 1) * PARTS // 2]:
            for copy in part:
                copy.wait_recv()

    def start_halo(phase, turn, a):
        for condition, copy in halo(phase, order[phase][turn], a):
            pl.when(condition)(copy.start)

    def hand_on(pg):
        for a in range(2):
            condition, copy = passed[*pg, a]

            @pl.when(condition)
            def _():
                pltpu.make_async_copy(copy.src_ref, copy.src_ref, relay_recv.at[pg]).wait()
                copy.start()

    def forward(pg):
        for a in range(2):
            condition, copy = seconds[*pg, a]

            @pl.when(condition)
            def _():
                halos[*pg, a][0][1].wait_recv()
                copy.start()

    def near(pg):
        for a in range(2):
            inside = comes(pg[1], 1) & ~seconds[*pg, a][0]
            pl.when(inside)(halos[*pg, a][0][1].wait_recv)
            shares[*pg, a][0].start()

    def middle(pg):
        diagonal(*pg)
        for a in range(2):
            shares[*pg, a][0].wait_recv()
        others(*pg, 2)

    def far(pg):
        for a in range(2):
            pl.when(comes(pg[1], 2))(halos[*pg, a][1][1].wait_recv)
            shares[*pg, a][1].start()
        for a in range(2):
            shares[*pg, a][1].wait_recv()
        others(*pg, 4)

    def start_give(pg):
        finish(*pg)
        for copy in gives[pg][1]:
            copy.start()

    kv_a, qd_a, kv_b, qd_b = groups
    issue(5)
    arrive(0, 0, 0)
    start_halo(0, 0, 0)
    issue(2)
    arrive(0, 0, 1)
    theirs, mine = held.at[0, 0, 0], held.at[0, 1, 0]
    for p in range(PLANES):
        numbers = theirs[p, 2 * TOK :, :]
        mine[p, 2 * TOK :, :] = numbers
        row = numbers.astype(jnp.float32)[0:1, :]
        seg_rows[p * TOK : (p + 1) * TOK, :] = jnp.broadcast_to(row, (TOK, TOK)).T
    start_halo(0, 0, 1)
    issue(1)
    hand_on(kv_a)
    issue(2)
    arrive(0, 1, 0)
    start_halo(0, 1, 0)
    issue(1)
    arrive(0, 1, 1)
    start_halo(0, 1, 1)

    issue(1)
    forward(kv_a)
    near(kv_a)
    hand_on(qd_a)
    middle(kv_a)
    issue(2)
    arrive(1, 0, 0)
    start_halo(1, 0, 0)
    far(kv_a)
    start_give(kv_a)
    arrive(1, 0, 1)
    start_halo(1, 0, 1)
    issue(2)

    forward(qd_a)
    near(qd_a)
    middle(qd_a)
    hand_on(kv_b)
    hand_on(qd_b)
    issue(1)
    arrive(1, 1, 0)
    start_halo(1, 1, 0)
    far(qd_a)
    start_give(qd_a)
    issue(2)

    arrive(1, 1, 1)
    start_halo(1, 1, 1)
    forward(kv_b)
    near(kv_b)
    middle(kv_b)
    forward(qd_b)
    issue(6 * PARTS - len(issued), limited=False)
    far(kv_b)
    start_give(kv_b)
    issue(PARTS, limited=False)

    near(qd_b)
    middle(qd_b)
    far(qd_b)
    start_give(qd_b)
    issue(PARTS, limited=False)

    left(len(queue))
    for half in halves:
        for copy in shares[half]:
            copy.wait_send()
        for condition, copy in halos[half] + [passed[half], seconds[half]]:
            pl.when(condition)(copy.wait_send)
    for pg in groups:
        parts, own = gives[pg]
        for part in parts:
            for copy in part:
                copy.wait_recv()
        for copy in own:
            copy.wait()


def hand_over(*refs):
    ins, outs, (here, sems) = refs[:4], refs[4:8], refs[8:]
    arriving = [pltpu.make_async_copy(ins[i], here.at[i], sems.at[0, i]) for i in range(4)]
    leaving = [pltpu.make_async_copy(here.at[i], outs[i], sems.at[1, i]) for i in range(4)]
    for copy in arriving:
        copy.start()
    for i in range(4):
        arriving[i].wait()
        leaving[i].start()
    for copy in leaving:
        copy.wait()


def shards(grps, queries, keys, values, out_grad, segment):
    tokens, features = queries.shape
    shape = jax.ShapeDtypeStruct((tokens, features), jnp.bfloat16)
    anywhere = pl.BlockSpec(memory_space=pl.ANY)
    dma = pltpu.SemaphoreType.DMA
    results = pl.pallas_call(
        functools.partial(kernel, grps),
        out_shape=(shape,) * 4,
        in_specs=[anywhere] * 5,
        out_specs=[anywhere] * 4,
        scratch_shapes=[
            pltpu.VMEM((2, 2, REACH + 1, PLANES, CHUNK, DH), jnp.bfloat16),
            pltpu.VMEM((2, 2, PLANES - 1, CHUNK, DH), jnp.bfloat16),
            pltpu.VMEM((2, 2, 2, PLANES, TOK, DH), jnp.bfloat16),
            pltpu.VMEM((2, 2, BLOCK, DH), jnp.float32),
            pltpu.VMEM((BLOCK, TOK), jnp.float32),
            dma((2, 2, PLANES, 2)),
            dma((2, 2, PARTS, 3)),
            dma((2, 2, PARTS, 3)),
            dma((2, 2, 2, 2)),
            dma((2, 2, 2, 2)),
            dma((2, 2, 2, 2)),
            dma((2, 2, 2, 2)),
            dma((2, 2, PARTS, 3)),
            dma((2, 2, PARTS, 3)),
            dma((2, 2, 2)),
            pltpu.VMEM((2, 2, CHUNK, DH), jnp.bfloat16),
            dma((2, 2, 2, SIDE)),
            dma((2, 2)),
            dma((2, 2)),
            dma((2, 2, 2)),
            dma(()),
            pltpu.VMEM((1, TOK), jnp.int32),
        ],
        compiler_params=pltpu.CompilerParams(
            collective_id=0, has_side_effects=True, vmem_limit_bytes=60 << 20
        ),
        cost_estimate=pl.CostEstimate(
            flops=2 * 2 * 10 * 4 * BLOCK * BLOCK * DH,
            bytes_accessed=8 * tokens * features * 2,
            transcendentals=2 * 10 * BLOCK * BLOCK,
        ),
    )(queries, keys, values, out_grad, segment.reshape(1, tokens))
    return pl.pallas_call(
        hand_over,
        out_shape=(shape,) * 4,
        in_specs=[anywhere] * 4,
        out_specs=[anywhere] * 4,
        scratch_shapes=[pltpu.VMEM((4, tokens, features), jnp.bfloat16), dma((2, 4))],
        compiler_params=pltpu.CompilerParams(vmem_limit_bytes=60 << 20),
    )(*results)


def solution(mesh):
    rows = P(("grp", "blk", "head"), None)
    return jax.shard_map(
        functools.partial(shards, mesh.shape["grp"]),
        mesh=mesh,
        in_specs=(rows, rows, rows, rows, P(("grp", "blk", "head"))),
        out_specs=(rows,) * 4,
        check_vma=False,
    )
```
